32 devices in a mesh: blk: 8 (over z, x), sub: 4 (over y, core).
Axes of the slice: x: 2, y: 2, z: 4, core: 2. Of those that a mesh axis runs over, the one named last changes fastest.
Arguments:
- features: bfloat16 [16, 65536], P(None, ('blk', 'sub')), may hold values from -6 to 6
- adjacency: bfloat16 [512, 8, 128, 128], P(('blk', 'sub')), may hold values from 0.049804688 to 2
- col_tiles: int32 [512, 8], P(('blk', 'sub')), may hold values from 0 to 511, as said below
- match_one: int32 [256, 128], replicated, may hold values from 0 to 127, each once within a row
- match_two: int32 [128, 128], replicated, may hold values from 0 to 127, each once within a row
Outputs:
- coarse_adjacency: bfloat16 [128, 8, 128, 128], P(('blk', 'sub'))
- coarse_features: bfloat16 [16, 16384], P(None, ('blk', 'sub'))
The draws below stay inside these ranges and needn't reach their ends.
Inputs may be any that keep to these rules, and one draw needn't show every extreme that they name: `col_tiles`: for each slot k, the two tiles t and t + 64 of a level-one pair ((t // 64) even) name column tiles that differ by 0 or 64; with that difference cleared, the tiles t and t + 16 ((t // 16) even, (t // 64) even) name column tiles that differ by 0 or 16. `match_one`: each row is a matching of the high tile's rows onto the low tile's rows. `match_two`: each row is a matching of the high tile's rows onto the low tile's rows.
All inputs are finite; a program needn't handle non-finite values.
Results may differ from the reference program's by a relative error of at most 0.0053.
Values may be sent and summed in bfloat16 or wider, within the bound.
No kernel may reach another device: no remote copies, remote signals or barrier semaphores. Data moves between devices by JAX's collectives and lax.ppermute only.
A program may use at most 64 MiB of HBM per device.

```python
import math
import jax
import jax.numpy as jnp
from jax import lax

FEAT = 16
TILE = 128
NBR = 8
TPD = 16
SPAN = 64
NT = 512
ROWS = 65536
PAIRS = 256
GROUPS = 128


def draw_col_tiles(key, part):
    key_group, key_sub, key_blk = jax.random.split(key, 3)
    tile_ids = jnp.arange(NT, dtype=jnp.int32)
    pair_ids = tile_ids // (2 * SPAN) * SPAN + tile_ids % SPAN
    group_ids = pair_ids // (2 * TPD) * TPD + pair_ids % TPD
    targets = jax.random.randint(key_group, (GROUPS, NBR), 0, GROUPS, dtype=jnp.int32)
    targets = targets.at[0, 0].set(GROUPS - 1).at[0, 1].set(0)
    sub_bits = jax.random.randint(key_sub, (PAIRS, NBR), 0, 2, dtype=jnp.int32)
    sub_bits = sub_bits.at[0, 0].set(1).at[0, 1].set(0)
    blk_bits = jax.random.randint(key_blk, (NT, NBR), 0, 2, dtype=jnp.int32)
    blk_bits = blk_bits.at[0, 0].set(1).at[0, 1].set(0)
    target_pairs = targets // TPD * 2 * TPD + targets % TPD
    base_tiles = target_pairs // SPAN * 2 * SPAN + target_pairs % SPAN
    return base_tiles[group_ids] + sub_bits[pair_ids] * TPD + blk_bits * SPAN


def shard_levels(key, extent, shards, low, top_value):
    gain, own = 1.0, jax.random.fold_in(key, 6)
    for position, shards_of in shards:
        steps = jnp.exp(jax.random.uniform(jax.random.fold_in(own, position), (shards_of,), jnp.float32, low / len(shards), top_value / len(shards)))
        gain = gain * jnp.repeat(steps, extent[position] // shards_of).reshape([-1 if axis == position else 1 for axis in range(len(extent))])
    return gain


def bell_draw(stream_key, shape, width, bound, cuts=(), held_as=jnp.bfloat16):
    drawn = width * jax.random.normal(stream_key, shape, jnp.float32)
    if cuts:
        drawn = drawn * shard_levels(stream_key, shape, cuts, -0.22, 0.18)
    return jnp.clip(drawn, -bound, bound).astype(held_as)


def setup_inputs(seed: int = 0) -> dict:
    splits = jax.random.split(jax.random.key(seed), 6)
    return {
        "features": bell_draw(splits[0], (FEAT, ROWS), 1.0, 6.0, ((1, 32),)),
        "adjacency": jnp.clip(jnp.exp(math.log(2.0) - 3.6927934 * jax.random.uniform(splits[1], (NT, NBR, TILE, TILE), jnp.float32) ** shard_levels(splits[1], (NT, NBR, TILE, TILE), ((0, 32),), -0.2, 0.2)), 0.049804688, 2.0).astype(jnp.bfloat16),
        "col_tiles": draw_col_tiles(jax.random.fold_in(splits[5], 71), 0),
        "match_one": jax.vmap(lambda own: jax.random.permutation(own, TILE))(jax.random.split(splits[3], PAIRS)).reshape((PAIRS, TILE)).astype(jnp.int32),
        "match_two": jax.vmap(lambda own: jax.random.permutation(own, TILE))(jax.random.split(splits[4], GROUPS)).reshape((GROUPS, TILE)).astype(jnp.int32),
    }


def one_hot(row_maps):
    return (row_maps[..., :, None] == jnp.arange(TILE, dtype=jnp.int32)).astype(jnp.bfloat16)


def pair_of(column_ids):
    return (column_ids // (2 * SPAN)) * SPAN + column_ids % SPAN


def reference(features, adjacency, col_tiles, match_one, match_two):
    positions = jnp.arange(TILE, dtype=jnp.int32)

    def first_map(column_ids):
        upper = (column_ids // SPAN) % 2 == 1
        return jnp.where(upper[..., None], match_one[pair_of(column_ids)], positions)

    def second_map(column_ids):
        pair_index = pair_of(column_ids)
        group_index = (pair_index // (2 * TPD)) * TPD + pair_index % TPD
        upper = (column_ids // TPD) % 2 == 1
        return jnp.where(upper[..., None], match_two[group_index], positions)

    def column_side(blocks, column_ids, mapper):
        return jnp.einsum('kab,kbc->kac', blocks.astype(jnp.float32),
                          one_hot(mapper(column_ids)).astype(jnp.float32))

    feats = features.reshape(FEAT, NT, TILE)

    def level_one(pair_index):
        low_tile = (pair_index // SPAN) * 2 * SPAN + pair_index % SPAN
        high_tile = low_tile + SPAN
        rows_hot = one_hot(match_one[pair_index]).astype(jnp.float32)
        low_term = column_side(adjacency[low_tile], col_tiles[low_tile], first_map)
        high_cols = column_side(adjacency[high_tile], col_tiles[high_tile], first_map)
        high_term = jnp.einsum('ba,kbc->kac', rows_hot, high_cols)
        blocks = (low_term + high_term).astype(jnp.bfloat16)
        low_feat = feats[:, low_tile].astype(jnp.float32)
        high_feat = jnp.dot(feats[:, high_tile].astype(jnp.float32), rows_hot, precision=lax.Precision.HIGHEST)
        merged = (low_feat + high_feat).astype(jnp.bfloat16)
        low_cols = col_tiles[low_tile]
        coarse_cols = low_cols - ((low_cols // SPAN) % 2) * SPAN
        return blocks, merged, coarse_cols

    tiles_one, feats_one, cols_one = lax.map(level_one, jnp.arange(PAIRS, dtype=jnp.int32))

    def level_two(out_index):
        device_index = out_index // (TPD // 4)
        piece_index = out_index % (TPD // 4)
        sub_bit = device_index % 2
        blk_bit = (device_index * TPD // SPAN) % 2
        low_tile = device_index * TPD - sub_bit * TPD - blk_bit * SPAN + 4 * piece_index + 2 * blk_bit + sub_bit
        pair_low = pair_of(low_tile)
        pair_high = pair_low + TPD
        group_index = (pair_low // (2 * TPD)) * TPD + pair_low % TPD
        rows_hot = one_hot(match_two[group_index]).astype(jnp.float32)
        low_term = column_side(tiles_one[pair_low], cols_one[pair_low], second_map)
        high_cols = column_side(tiles_one[pair_high], cols_one[pair_high], second_map)
        high_term = jnp.einsum('ba,kbc->kac', rows_hot, high_cols)
        blocks = (low_term + high_term).astype(jnp.bfloat16)
        high_feat = jnp.dot(feats_one[pair_high].astype(jnp.float32), rows_hot, precision=lax.Precision.HIGHEST)
        merged = (feats_one[pair_low].astype(jnp.float32) + high_feat).astype(jnp.bfloat16)
        return blocks, merged

    tiles_two, feats_two = lax.map(level_two, jnp.arange(GROUPS, dtype=jnp.int32))
    coarse_features = jnp.transpose(feats_two, (1, 0, 2)).reshape(FEAT, GROUPS * TILE)
    return tiles_two, coarse_features
```

```python
import functools

import jax
import jax.numpy as jnp
from jax import lax
from jax.experimental import pallas as pl
from jax.experimental.pallas import tpu as pltpu
from jax.sharding import PartitionSpec as P


def swapped(value, axis):
    pairs = [(source, source ^ 1) for source in range(lax.axis_size(axis))]
    return lax.ppermute(value, axis, pairs)


def split_by(value, size):
    if size & (size - 1) == 0:
        return value >> (size.bit_length() - 1), value & (size - 1)
    return value // size, value % size


def merged_kernel(
    first, slots, span, count, scal, own_cols, other_cols, own, other, own_feat, other_feat,
    match_one, match_two, *rest
):
    (tile_out, feat_out, one_rows, two_rows) = rest
    width = own.shape[-1]
    tile = 4 * (first + pl.program_id(0)) + 2 * scal[0] + scal[1]
    lanes = lax.broadcasted_iota(jnp.int32, (1, width), 1)

    def put(row, column_id):
        block, inside = split_by(column_id, span)
        pair_block, high_one = split_by(block, 2)
        sub, place = split_by(inside, count)
        sub_pair, high_two = split_by(sub, 2)
        pair = pair_block * span + inside
        group = pair_block * (span // 2) + sub_pair * count + place
        one_rows[pl.ds(row, 1), :] = jnp.where(high_one == 1, match_one[pl.ds(pair, 1), :], lanes)
        two_rows[pl.ds(row, 1), :] = jnp.where(high_two == 1, match_two[pl.ds(group, 1), :], lanes)

    for slot in range(slots):
        put(slot, own_cols[tile, slot])
        put(slots + slot, other_cols[tile, slot])
    put(2 * slots, scal[2] + tile)
    put(2 * slots + 1, scal[3] + tile)
    maps = jnp.take_along_axis(two_rows[...], one_rows[...], axis=1)
    down = maps.T
    across = lax.broadcasted_iota(jnp.int32, (width, width), 1)
    along = lax.broadcasted_iota(jnp.int32, (width, width), 0)

    def columns(row):
        return (down[:, row : row + 1] == across).astype(jnp.bfloat16)

    def dot(a, b):
        return jnp.dot(a, b, preferred_element_type=jnp.float32)

    own_rows = (maps[2 * slots : 2 * slots + 1, :] == along).astype(jnp.bfloat16)
    other_rows = (maps[2 * slots + 1 : 2 * slots + 2, :] == along).astype(jnp.bfloat16)
    for pair in range(slots // 2):
        left, right = 2 * pair, 2 * pair + 1
        own_two = dot(own_rows, jnp.concatenate([own[0, left], own[0, right]], 1)).astype(jnp.bfloat16)
        other_two = dot(other_rows, jnp.concatenate([other[0, left], other[0, right]], 1)).astype(
            jnp.bfloat16
        )
        for half, slot in enumerate((left, right)):
            lhs = jnp.concatenate(
                [
                    own_two[:, half * width : (half + 1) * width],
                    other_two[:, half * width : (half + 1) * width],
                ],
                1,
            )
            rhs = jnp.concatenate([columns(slot), columns(slots + slot)], 0)
            total = dot(lhs, rhs).astype(jnp.bfloat16)
            if feat_out is None:
                tile_out[0, slot * width : (slot + 1) * width, :] = total
            else:
                tile_out[0, slot] = total
    feats = dot(
        jnp.concatenate([own_feat[...], other_feat[...]], 1),
        jnp.concatenate([columns(2 * slots), columns(2 * slots + 1)], 0),
    ).astype(jnp.bfloat16)
    if feat_out is None:
        tile_out[0, slots * width :, :] = feats
    else:
        feat_out[...] = feats


def packed_kernel(first, slots, span, count, *refs):
    merged_kernel(first, slots, span, count, *refs[:9], refs[9], None, *refs[10:])


def merged(first, tiles, packed, span, scal, own_cols, other_cols, adjacency, other, feats, other_feats,
           match_one, match_two):
    count, slots, width = adjacency.shape[:3]
    feat_count = feats.shape[0]
    whole = lambda array: pl.BlockSpec(array.shape, lambda i, *_: (0, 0))
    tile_of = lambda i, scal: 4 * (first + i) + 2 * scal[0] + scal[1]
    in_specs = [
        pl.BlockSpec((1, slots, width, width), lambda i, scal, *_: (tile_of(i, scal), 0, 0, 0)),
        pl.BlockSpec((1, slots, width, width), lambda i, *_: (i, 0, 0, 0)),
        pl.BlockSpec((feat_count, width), lambda i, scal, *_: (0, tile_of(i, scal))),
        pl.BlockSpec((feat_count, width), lambda i, scal, *_: (0, tile_of(i, scal))),
        whole(match_one),
        whole(match_two),
    ]
    if packed:
        body = packed_kernel
        depth = slots * width + feat_count
        out_shape = jax.ShapeDtypeStruct((tiles, depth, width), jnp.bfloat16)
        out_specs = pl.BlockSpec((1, depth, width), lambda i, *_: (i, 0, 0))
    else:
        body = merged_kernel
        out_shape = (
            jax.ShapeDtypeStruct((tiles, slots, width, width), jnp.bfloat16),
            jax.ShapeDtypeStruct((feat_count, tiles * width), jnp.bfloat16),
        )
        out_specs = (
            pl.BlockSpec((1, slots, width, width), lambda i, *_: (i, 0, 0, 0)),
            pl.BlockSpec((feat_count, width), lambda i, *_: (0, i)),
        )
    map_rows = -(-(2 * slots + 2) // 8) * 8
    return pl.pallas_call(
        functools.partial(body, first, slots, span, count),
        out_shape=out_shape,
        grid_spec=pltpu.PrefetchScalarGridSpec(
            num_scalar_prefetch=3,
            grid=(tiles,),
            in_specs=in_specs,
            out_specs=out_specs,
            scratch_shapes=[pltpu.VMEM((map_rows, width), jnp.int32)] * 2,
        ),
        compiler_params=pltpu.CompilerParams(vmem_limit_bytes=32 * 2**20),
        cost_estimate=pl.CostEstimate(
            flops=tiles * slots * 8 * width**3,
            bytes_accessed=tiles * slots * width * width * 6,
            transcendentals=0,
        ),
    )(scal, own_cols, other_cols, adjacency, other, feats, other_feats, match_one, match_two)


def add_kernel(slots, arrived, tiles_in, feats_in, tiles_out, feats_out):
    width = arrived.shape[-1]
    for slot in range(slots):
        tiles_out[0, slot] = (
            tiles_in[0, slot].astype(jnp.float32)
            + arrived[0, slot * width : (slot + 1) * width, :].astype(jnp.float32)
        ).astype(jnp.bfloat16)
    feats_out[...] = (
        feats_in[...].astype(jnp.float32) + arrived[0, slots * width :, :].astype(jnp.float32)
    ).astype(jnp.bfloat16)


def added(first, arrived, tiles, feats):
    slots, width = tiles.shape[1:3]
    feat_count = feats.shape[0]
    tile_spec = pl.BlockSpec((1, slots, width, width), lambda i: (first + i, 0, 0, 0))
    feat_spec = pl.BlockSpec((feat_count, width), lambda i: (0, first + i))
    return pl.pallas_call(
        functools.partial(add_kernel, slots),
        out_shape=(
            jax.ShapeDtypeStruct(tiles.shape, tiles.dtype),
            jax.ShapeDtypeStruct(feats.shape, feats.dtype),
        ),
        grid=(arrived.shape[0],),
        in_specs=[
            pl.BlockSpec((1,) + arrived.shape[1:], lambda i: (i, 0, 0)),
            tile_spec,
            feat_spec,
        ],
        out_specs=(tile_spec, feat_spec),
        input_output_aliases={1: 0, 2: 1},
        compiler_params=pltpu.CompilerParams(vmem_limit_bytes=32 * 2**20),
        cost_estimate=pl.CostEstimate(
            flops=arrived.size, bytes_accessed=arrived.size * 6, transcendentals=0
        ),
    )(arrived, tiles, feats)


def per_device(features, adjacency, col_tiles, match_one, match_two):
    count, slots, width = adjacency.shape[:3]
    quarter = count // 4
    sub_count = lax.axis_size("sub")
    span = sub_count * count
    blk_index = lax.axis_index("blk")
    sub_index = lax.axis_index("sub")
    own_first = (blk_index * sub_count + sub_index) * count
    other_first = (blk_index * sub_count + (sub_index ^ 1)) * count
    blk_bit = blk_index % 2
    sub_bit = sub_index % 2
    grid = adjacency.reshape(quarter, 2, 2, slots, width, width)

    def raw(first, tiles, row_bit):
        zero = jnp.int32(0)
        piece = lax.dynamic_slice(
            grid,
            (jnp.int32(first), row_bit, 1 - sub_bit, zero, zero, zero),
            (tiles, 1, 1, slots, width, width),
        )
        return swapped(piece.reshape(tiles, slots, width, width), "sub")

    cuts = [(0, 1), (1, 1), (2, 2)]
    other_cols = swapped(col_tiles, "sub")
    other_feats = swapped(features, "sub")
    others = [raw(first, tiles, 1 - blk_bit) for first, tiles in cuts]
    other_keep = raw(0, quarter, blk_bit)
    send_scal = jnp.stack([1 - blk_bit, sub_bit, own_first, other_first])
    keep_scal = jnp.stack([blk_bit, sub_bit, own_first, other_first])
    arrived = []
    for (first, tiles), other in zip(cuts, others):
        parcel = merged(
            first, tiles, True, span, send_scal, col_tiles, other_cols, adjacency, other, features,
            other_feats, match_one, match_two,
        )
        arrived.append(swapped(parcel, "blk"))
    tiles_out, feats_out = merged(
        0, quarter, False, span, keep_scal, col_tiles, other_cols, adjacency, other_keep, features,
        other_feats, match_one, match_two,
    )
    for (first, _), part in zip(cuts, arrived):
        tiles_out, feats_out = added(first, part, tiles_out, feats_out)
    return tiles_out, feats_out


def solution(mesh):
    placed = (
        P(None, ("blk", "sub")),
        P(("blk", "sub"), None, None, None),
        P(("blk", "sub"), None),
        P(),
        P(),
    )
    return jax.shard_map(
        per_device,
        mesh=mesh,
        in_specs=placed,
        out_specs=(P(("blk", "sub"), None, None, None), P(None, ("blk", "sub"))),
        check_vma=False,
    )
```

```python
import functools

import jax
import jax.numpy as jnp
from jax import lax
from jax.experimental import pallas as pl
from jax.experimental.pallas import tpu as pltpu
from jax.sharding import PartitionSpec as P

HALF = 16
LIMIT = 48 * 2**20
LIGHT = pl.CostEstimate(flops=1, bytes_accessed=1, transcendentals=0)
VMEM = pl.BlockSpec(memory_space=pltpu.VMEM)
HBM = pl.BlockSpec(memory_space=pltpu.HBM)
ANY = pl.BlockSpec(memory_space=pl.ANY)


def swapped(value, axis):
    pairs = [(source, source ^ 1) for source in range(lax.axis_size(axis))]
    return lax.ppermute(value, axis, pairs)


def in_vmem(value):
    return pltpu.with_memory_space_constraint(value, pltpu.VMEM)


def in_hbm(value):
    return pltpu.with_memory_space_constraint(value, pltpu.HBM)


def split_by(value, size):
    if size & (size - 1) == 0:
        return value >> (size.bit_length() - 1), value & (size - 1)
    return value // size, value % size


def tile_at(phase, piece, partner):
    blk_bit = lax.axis_index("blk") & 1
    sub_bit = lax.axis_index("sub") & 1
    row_bit = blk_bit if phase == 1 else 1 - blk_bit
    return 4 * piece + 2 * row_bit + (1 - sub_bit if partner else sub_bit)


def start(source, target, sem):
    copy = pltpu.make_async_copy(source, target, sem)
    copy.start()
    return copy


def compose_maps(pick, span, count, cols, one_table, two_table, one_rows, two_rows, out):
    slots = cols.shape[0]
    lanes = lax.broadcasted_iota(jnp.int32, (1, one_table.shape[-1]), 1)

    def put(row, column_id):
        block, inside = split_by(column_id, span)
        pair_block, high_one = split_by(block, 2)
        sub, place = split_by(inside, count)
        sub_pair, high_two = split_by(sub, 2)
        pair = pair_block * span + inside
        group = pair_block * (span // 2) + sub_pair * count + place
        one_rows[pl.ds(row, 1), :] = jnp.where(high_one == 1, one_table[pl.ds(pair, 1), :], lanes)
        two_rows[pl.ds(row, 1), :] = jnp.where(high_two == 1, two_table[pl.ds(group, 1), :], lanes)

    one_rows[...] = jnp.zeros_like(one_rows)
    two_rows[...] = jnp.zeros_like(two_rows)
    tile = tile_at(*pick)
    for slot in range(slots):
        put(slot, cols[slot, tile])
    put(slots, lax.axis_index("blk") * span + lax.axis_index("sub") * count + tile)
    maps = jnp.take_along_axis(two_rows[...], one_rows[...], axis=1)
    out[...] = maps.astype(jnp.float32).astype(out.dtype)


def merge_tile(slots, own, other, own_side, other_side, out):
    width = own.shape[-1]
    sides = lax.broadcasted_iota(jnp.int32, (width, width), 1).astype(jnp.float32)
    along = lax.broadcasted_iota(jnp.int32, (width, width), 0).astype(jnp.float32)
    across = jnp.concatenate([own_side[:HALF], other_side[:HALF]], 0).astype(jnp.float32)
    down = across.T

    def dot(a, b):
        return jnp.dot(a, b, preferred_element_type=jnp.float32)

    def columns(row):
        return jnp.concatenate(
            [
                (down[:, place : place + 1] == sides).astype(jnp.bfloat16)
                for place in (row, HALF + row)
            ],
            0,
        )

    own_rows = (across[slots : slots + 1, :] == along).astype(jnp.bfloat16)
    other_rows = (across[HALF + slots : HALF + slots + 1, :] == along).astype(jnp.bfloat16)
    for pair in range(slots // 2):
        both = [2 * pair, 2 * pair + 1]

        def moved(hot, ref):
            blocks = [ref[slot * width : (slot + 1) * width, :] for slot in both]
            return dot(hot, jnp.concatenate(blocks, 1)).astype(jnp.bfloat16)

        own_two = moved(own_rows, own)
        other_two = moved(other_rows, other)
        for half, slot in enumerate(both):
            part = slice(half * width, (half + 1) * width)
            lhs = jnp.concatenate([own_two[:, part], other_two[:, part]], 1)
            out[slot * width : (slot + 1) * width, :] = dot(lhs, columns(slot)).astype(out.dtype)
    feats = jnp.concatenate([own_side[HALF:], other_side[HALF:]], 1)
    out[slots * width :, :] = dot(feats, columns(slots)).astype(out.dtype)


def work_kernel(plan, refs):
    rows = plan.rows
    copies, small = [], []
    if plan.picks:
        adjacency, features, cols, match_one, match_two = [refs[at] for at in plan.sources]
        one_table, two_table, cols_here, one_rows, two_rows, sems = [refs[at] for at in plan.scratch]
        width = adjacency.shape[-1]
        small = [
            start(match_one, one_table, sems.at[0]),
            start(match_two, two_table, sems.at[1]),
            start(cols, cols_here, sems.at[2]),
        ]
        sides = []
        for i, (pick, (main, main_at, side, side_at)) in enumerate(zip(plan.picks, plan.targets)):
            tile = tile_at(*pick)
            lanes = pl.ds(pl.multiple_of(tile * width, width), width)
            sides.append(refs[side].at[pl.ds(side_at, HALF)])
            copies += [
                start(adjacency.at[tile], refs[main].at[pl.ds(main_at, rows)], sems.at[3 + 2 * i]),
                start(
                    features.at[:, lanes],
                    refs[side].at[pl.ds(side_at + HALF, features.shape[0])],
                    sems.at[4 + 2 * i],
                ),
            ]
    for i, (own, other) in enumerate(plan.merges):
        out = refs[plan.out].at[i]
        tiles = [refs[main].at[pl.ds(at, rows)] for main, at, _, _ in (own, other)]
        ends = [refs[side][at : at + plan.depth - rows, :] for _, _, side, at in (own, other)]
        merge_tile(rows // out.shape[-1], *tiles, *ends, out)
    for copy in small:
        copy.wait()
    for i, pick in enumerate(plan.picks):
        compose_maps(
            pick, plan.span, plan.count, cols_here, one_table, two_table, one_rows, two_rows,
            sides[i],
        )
    for copy in copies:
        copy.wait()


class Plan:
    pass


class Work:
    def __init__(self, features, adjacency, cols, match_one, match_two, span):
        self.sources = [in_hbm(x) for x in (adjacency, features, cols, match_one, match_two)]
        self.span = span
        self.own, self.other = {}, {}

    def run(self, merges=(), keys=(), leaving=(), apart=False, after=()):
        adjacency, features, cols, match_one, match_two = self.sources
        rows, width = adjacency.shape[1:]
        plan = Plan()
        plan.rows, plan.depth = rows, rows + HALF + features.shape[0]
        plan.span, plan.count = self.span, cols.shape[1]
        plan.picks = [(*key, True) for key in leaving] + [(*key, False) for key in keys]
        ins, specs, shapes, scratch = [], [], [], []

        def take(value, spec):
            for place, known in enumerate(ins):
                if known is value:
                    return place
            ins.append(value)
            specs.append(spec)
            return len(ins) - 1

        plan.sources = [take(value, HBM) for value in self.sources] if plan.picks else []
        plan.merges = [
            [
                (take(main, VMEM), at, take(side, VMEM), side_at)
                for main, at, side, side_at in (self.own[key], self.other[key])
            ]
            for key in merges
        ]
        for value in after:
            take(value, ANY)

        def give(depth):
            shapes.append(pltpu.VMEM((depth, width), adjacency.dtype))
            return len(ins) + len(shapes) - 1

        plan.out = len(ins)
        if merges:
            depth = rows + features.shape[0]
            shapes.append(pltpu.VMEM((len(merges), depth, width), adjacency.dtype))
        extra = plan.depth - rows
        if apart:
            side = give(len(leaving) * extra)
            plan.targets = [(give(rows), 0, side, i * extra) for i in range(len(leaving))]
        else:
            mains = [give(plan.depth) for _ in leaving]
            plan.targets = [(main, 0, main, rows) for main in mains]
        if keys:
            pack = give(len(keys) * plan.depth)
            plan.targets += [
                (pack, i * plan.depth, pack, i * plan.depth + rows) for i in range(len(keys))
            ]
        if plan.picks:
            scratch = [
                pltpu.VMEM(match_one.shape, jnp.int32),
                pltpu.VMEM(match_two.shape, jnp.int32),
                pltpu.SMEM(cols.shape, jnp.int32),
                pltpu.VMEM((HALF, width), jnp.int32),
                pltpu.VMEM((HALF, width), jnp.int32),
                pltpu.SemaphoreType.DMA((3 + 2 * len(plan.picks),)),
            ]
        plan.scratch = [len(ins) + len(shapes) + i for i in range(len(scratch))]
        outs = pl.pallas_call(
            lambda *refs: work_kernel(plan, refs),
            out_shape=shapes,
            in_specs=specs,
            out_specs=[VMEM] * len(shapes),
            scratch_shapes=scratch,
            compiler_params=pltpu.CompilerParams(vmem_limit_bytes=LIMIT),
            cost_estimate=LIGHT,
            name="work",
        )(*ins)
        made = {len(ins) + i: value for i, value in enumerate(outs)}
        crossed = {}
        for pick, (main, main_at, side, side_at) in zip(plan.picks, plan.targets):
            where = self.other if pick[2] else self.own
            for place in (main, side):
                if place not in crossed:
                    value = swapped(made[place], "sub") if pick[2] else made[place]
                    crossed[place] = in_vmem(value)
            where[pick[:2]] = (crossed[main], main_at, crossed[side], side_at)
        return outs[0]


def add_kernel(first, slots, arrived, kept, *rest):
    tiles_out, feats_out, tile_sum, feat_sum, sems = rest[-5:]
    width = arrived.shape[-1]
    rows = slots * width
    tiles = arrived.shape[0]
    copies = []
    for i in range(tiles):
        total = kept[first + i].astype(jnp.float32) + arrived[i].astype(jnp.float32)
        total = total.astype(jnp.bfloat16)
        tile_sum[i] = total[:rows]
        feat_sum[:, i * width : (i + 1) * width] = total[rows:]
        copies.append(
            pltpu.make_async_copy(tile_sum.at[i], tiles_out.at[first + i], sems.at[i])
        )
        copies[-1].start()
    copies.append(
        pltpu.make_async_copy(
            feat_sum, feats_out.at[:, pl.ds(first * width, tiles * width)], sems.at[tiles]
        )
    )
    copies[-1].start()
    for copy in copies:
        copy.wait()


def added(first, slots, feat_count, arrived, kept, before):
    tiles, depth, width = arrived.shape
    rows = slots * width
    quarter = kept.shape[0]
    shapes = (
        jax.ShapeDtypeStruct((quarter, rows, width), jnp.bfloat16),
        jax.ShapeDtypeStruct((feat_count, quarter * width), jnp.bfloat16),
    )
    before = [] if before is None else list(before)
    return pl.pallas_call(
        functools.partial(add_kernel, first, slots),
        out_shape=shapes,
        in_specs=[VMEM, VMEM] + [HBM] * len(before),
        out_specs=(HBM, HBM),
        scratch_shapes=[
            pltpu.VMEM((tiles, rows, width), jnp.bfloat16),
            pltpu.VMEM((feat_count, tiles * width), jnp.bfloat16),
            pltpu.SemaphoreType.DMA((tiles + 1,)),
        ],
        input_output_aliases={2: 0, 3: 1} if before else {},
        compiler_params=pltpu.CompilerParams(vmem_limit_bytes=LIMIT),
        cost_estimate=LIGHT,
        name="add",
    )(in_vmem(arrived), in_vmem(kept), *before)


def per_device(features, adjacency, col_tiles, match_one, match_two):
    count, slots, width = adjacency.shape[:3]
    feat_count = features.shape[0]
    quarter = count // 4
    span = lax.axis_size("sub") * count
    blocks = adjacency.reshape(count, slots * width, width)
    work = Work(features, blocks, col_tiles.T, match_one, match_two, span)

    send = [(0, piece) for piece in range(quarter)]
    keep = [(1, piece) for piece in range(quarter)]
    first = work.run(leaving=send[:1])
    work.run(keys=send[:2], leaving=send[1:2], after=[first])
    more = {1: send[2:], 2: keep}
    arrived = []
    after = []
    for piece in range(quarter):
        new = more.get(piece, [])
        parcel = work.run(
            merges=send[piece : piece + 1], keys=new, leaving=new, apart=bool(new), after=after
        )
        arrived.append(swapped(parcel, "blk"))
        after = [parcel] + arrived[piece - 1 : piece] * (piece >= 1)
    kept = work.run(merges=keep, after=[parcel])
    out = None
    for piece, part in enumerate(arrived):
        out = added(piece, slots, feat_count, part, kept, out)
    return out[0].reshape(quarter, slots, width, width), out[1]


def solution(mesh):
    placed = (
        P(None, ("blk", "sub")),
        P(("blk", "sub"), None, None, None),
        P(("blk", "sub"), None),
        P(),
        P(),
    )
    return jax.shard_map(
        per_device,
        mesh=mesh,
        in_specs=placed,
        out_specs=(P(("blk", "sub"), None, None, None), P(None, ("blk", "sub"))),
        check_vma=False,
    )
```

```python
import functools

import jax
import jax.numpy as jnp
from jax import lax
from jax.experimental import pallas as pl
from jax.experimental.pallas import tpu as pltpu
from jax.sharding import PartitionSpec as P

HALF = 16
PARTS = 4
LIMIT = 48 * 2**20
LIGHT = pl.CostEstimate(flops=1, bytes_accessed=1, transcendentals=0)
VMEM = pl.BlockSpec(memory_space=pltpu.VMEM)
HBM = pl.BlockSpec(memory_space=pltpu.HBM)
ANY = pl.BlockSpec(memory_space=pl.ANY)


def swapped(value, axis):
    pairs = [(source, source ^ 1) for source in range(lax.axis_size(axis))]
    return lax.ppermute(value, axis, pairs)


def in_vmem(value):
    return pltpu.with_memory_space_constraint(value, pltpu.VMEM)


def in_hbm(value):
    return pltpu.with_memory_space_constraint(value, pltpu.HBM)


def split_by(value, size):
    if size & (size - 1) == 0:
        return value >> (size.bit_length() - 1), value & (size - 1)
    return value // size, value % size


def tile_at(phase, piece, partner):
    blk_bit = lax.axis_index("blk") & 1
    sub_bit = lax.axis_index("sub") & 1
    row_bit = blk_bit if phase == 1 else 1 - blk_bit
    return 4 * piece + 2 * row_bit + (1 - sub_bit if partner else sub_bit)


def start(source, target, sem):
    copy = pltpu.make_async_copy(source, target, sem)
    copy.start()
    return copy


def compose_maps(pick, span, count, cols, one_table, two_table, one_rows, two_rows, out):
    slots = cols.shape[0]
    lanes = lax.broadcasted_iota(jnp.int32, (1, one_table.shape[-1]), 1)

    def put(row, column_id):
        block, inside = split_by(column_id, span)
        pair_block, high_one = split_by(block, 2)
        sub, place = split_by(inside, count)
        sub_pair, high_two = split_by(sub, 2)
        pair = pair_block * span + inside
        group = pair_block * (span // 2) + sub_pair * count + place
        one_rows[pl.ds(row, 1), :] = jnp.where(high_one == 1, one_table[pl.ds(pair, 1), :], lanes)
        two_rows[pl.ds(row, 1), :] = jnp.where(high_two == 1, two_table[pl.ds(group, 1), :], lanes)

    one_rows[...] = jnp.zeros_like(one_rows)
    two_rows[...] = jnp.zeros_like(two_rows)
    tile = tile_at(*pick)
    for slot in range(slots):
        put(slot, cols[slot, tile])
    put(slots, lax.axis_index("blk") * span + lax.axis_index("sub") * count + tile)
    maps = jnp.take_along_axis(two_rows[...], one_rows[...], axis=1)
    out[...] = maps.astype(jnp.float32).astype(out.dtype)


def merge_tile(slots, own, other, own_side, other_side, out):
    width = own.shape[-1]
    along = lax.broadcasted_iota(jnp.int32, (width, width), 0).astype(jnp.float32)
    own_maps, other_maps = (x[:HALF].astype(jnp.float32) for x in (own_side, other_side))

    def hot(maps, row):
        return (maps[row : row + 1, :] == along).astype(jnp.bfloat16)

    def columns(row):
        return jnp.concatenate([hot(own_maps, row), hot(other_maps, row)], 1)

    def across(value, row):
        return lax.dot_general(
            value, columns(row), (((1,), (1,)), ((), ())), preferred_element_type=jnp.float32
        )

    def moved(rows_hot, tile, pair):
        blocks = [tile[slot * width : (slot + 1) * width, :] for slot in (2 * pair, 2 * pair + 1)]
        value = jnp.dot(
            rows_hot, jnp.concatenate(blocks, 1), preferred_element_type=jnp.float32
        ).astype(jnp.bfloat16)
        return [value[:, :width], value[:, width:]]

    own_rows, other_rows = hot(own_maps, slots), hot(other_maps, slots)
    rows_done = []
    for pair in range(slots // 2):
        halves = moved(own_rows, own, pair), moved(other_rows, other, pair)
        rows_done += [jnp.concatenate(both, 1) for both in zip(*halves)]
    for slot, value in enumerate(rows_done):
        out[slot * width : (slot + 1) * width, :] = across(value, slot).astype(out.dtype)
    feats = jnp.concatenate([own_side[HALF:], other_side[HALF:]], 1)
    out[slots * width :, :] = across(feats, slots).astype(out.dtype)


def work_kernel(plan, refs):
    rows = plan.rows
    copies, small = [], []
    if plan.picks:
        adjacency, features, cols, match_one, match_two = [refs[at] for at in plan.sources]
        one_table, two_table, cols_here, one_rows, two_rows, sems = [refs[at] for at in plan.scratch]
        width = adjacency.shape[-1]
        small = [
            start(match_one, one_table, sems.at[0]),
            start(match_two, two_table, sems.at[1]),
            start(cols, cols_here, sems.at[2]),
        ]
        sides = []
        for i, (pick, (main, main_at, side, side_at)) in enumerate(zip(plan.picks, plan.targets)):
            tile = tile_at(*pick)
            lanes = pl.ds(pl.multiple_of(tile * width, width), width)
            sides.append(refs[side].at[pl.ds(side_at, HALF)])
            copies += [
                start(adjacency.at[tile], refs[main].at[pl.ds(main_at, rows)], sems.at[3 + 2 * i]),
                start(
                    features.at[:, lanes],
                    refs[side].at[pl.ds(side_at + HALF, features.shape[0])],
                    sems.at[4 + 2 * i],
                ),
            ]
    for i, (own, other) in enumerate(plan.merges):
        out = refs[plan.out].at[i]
        tiles = [refs[main].at[pl.ds(at, rows)] for main, at, _, _ in (own, other)]
        ends = [refs[side][at : at + plan.depth - rows, :] for _, _, side, at in (own, other)]
        merge_tile(rows // out.shape[-1], *tiles, *ends, out)
    for copy in small:
        copy.wait()
    for i, pick in enumerate(plan.picks):
        compose_maps(
            pick, plan.span, plan.count, cols_here, one_table, two_table, one_rows, two_rows,
            sides[i],
        )
    for copy in copies:
        copy.wait()


class Plan:
    pass


class Work:
    def __init__(self, features, adjacency, cols, match_one, match_two, span):
        self.sources = [in_hbm(x) for x in (adjacency, features, cols, match_one, match_two)]
        self.span = span
        self.own, self.other = {}, {}

    def run(self, merges=(), keys=(), leaving=(), apart=False, after=()):
        adjacency, features, cols, match_one, match_two = self.sources
        rows, width = adjacency.shape[1:]
        plan = Plan()
        plan.rows, plan.depth = rows, rows + HALF + features.shape[0]
        plan.span, plan.count = self.span, cols.shape[1]
        plan.picks = [(*key, True) for key in leaving] + [(*key, False) for key in keys]
        ins, specs, shapes, scratch = [], [], [], []

        def take(value, spec):
            for place, known in enumerate(ins):
                if known is value:
                    return place
            ins.append(value)
            specs.append(spec)
            return len(ins) - 1

        plan.sources = [take(value, HBM) for value in self.sources] if plan.picks else []
        plan.merges = [
            [
                (take(main, VMEM), at, take(side, VMEM), side_at)
                for main, at, side, side_at in (self.own[key], self.other[key])
            ]
            for key in merges
        ]
        for value in after:
            take(value, ANY)

        def give(depth):
            shapes.append(pltpu.VMEM((depth, width), adjacency.dtype))
            return len(ins) + len(shapes) - 1

        plan.out = len(ins)
        if merges:
            depth = rows + features.shape[0]
            shapes.append(pltpu.VMEM((len(merges), depth, width), adjacency.dtype))
        extra = plan.depth - rows
        if apart:
            side = give(len(leaving) * extra)
            plan.targets = [(give(rows), 0, side, i * extra) for i in range(len(leaving))]
        else:
            mains = [give(plan.depth) for _ in leaving]
            plan.targets = [(main, 0, main, rows) for main in mains]
        if keys:
            pack = give(len(keys) * plan.depth)
            plan.targets += [
                (pack, i * plan.depth, pack, i * plan.depth + rows) for i in range(len(keys))
            ]
        if plan.picks:
            scratch = [
                pltpu.VMEM(match_one.shape, jnp.int32),
                pltpu.VMEM(match_two.shape, jnp.int32),
                pltpu.SMEM(cols.shape, jnp.int32),
                pltpu.VMEM((HALF, width), jnp.int32),
                pltpu.VMEM((HALF, width), jnp.int32),
                pltpu.SemaphoreType.DMA((3 + 2 * len(plan.picks),)),
            ]
        plan.scratch = [len(ins) + len(shapes) + i for i in range(len(scratch))]
        outs = pl.pallas_call(
            lambda *refs: work_kernel(plan, refs),
            out_shape=shapes,
            in_specs=specs,
            out_specs=[VMEM] * len(shapes),
            scratch_shapes=scratch,
            compiler_params=pltpu.CompilerParams(vmem_limit_bytes=LIMIT),
            cost_estimate=LIGHT,
            name="work",
        )(*ins)
        made = {len(ins) + i: value for i, value in enumerate(outs)}
        crossed = {}
        for pick, (main, main_at, side, side_at) in zip(plan.picks, plan.targets):
            where = self.other if pick[2] else self.own
            for place in (main, side):
                if place not in crossed:
                    value = swapped(made[place], "sub") if pick[2] else made[place]
                    crossed[place] = in_vmem(value)
            where[pick[:2]] = (crossed[main], main_at, crossed[side], side_at)
        return outs[0]


def add_kernel(first, slots, arrived, kept, *rest):
    tiles_out, feats_out, tile_sum, feat_sum, sems = rest[-5:]
    width = arrived.shape[-1]
    rows = slots * width
    tiles = arrived.shape[0]
    part = rows // PARTS

    def total(i, here):
        value = kept[first + i, here].astype(jnp.float32) + arrived[i, here].astype(jnp.float32)
        return value.astype(jnp.bfloat16)

    for i in range(tiles):
        feat_sum[:, i * width : (i + 1) * width] = total(i, slice(rows, None))
    copies = [
        start(feat_sum, feats_out.at[:, pl.ds(first * width, tiles * width)], sems.at[tiles * PARTS])
    ]
    for i in range(tiles):
        for at in range(PARTS):
            tile_sum[i, at * part : (at + 1) * part] = total(i, slice(at * part, (at + 1) * part))
            here = pl.ds(at * part, part)
            copies.append(
                start(
                    tile_sum.at[i, here], tiles_out.at[first + i, here], sems.at[i * PARTS + at]
                )
            )
    for copy in copies:
        copy.wait()


def added(first, slots, feat_count, arrived, kept, before):
    tiles, depth, width = arrived.shape
    rows = slots * width
    quarter = kept.shape[0]
    shapes = (
        jax.ShapeDtypeStruct((quarter, rows, width), jnp.bfloat16),
        jax.ShapeDtypeStruct((feat_count, quarter * width), jnp.bfloat16),
    )
    before = [] if before is None else list(before)
    return pl.pallas_call(
        functools.partial(add_kernel, first, slots),
        out_shape=shapes,
        in_specs=[VMEM, VMEM] + [HBM] * len(before),
        out_specs=(HBM, HBM),
        scratch_shapes=[
            pltpu.VMEM((tiles, rows, width), jnp.bfloat16),
            pltpu.VMEM((feat_count, tiles * width), jnp.bfloat16),
            pltpu.SemaphoreType.DMA((tiles * PARTS + 1,)),
        ],
        input_output_aliases={2: 0, 3: 1} if before else {},
        compiler_params=pltpu.CompilerParams(vmem_limit_bytes=LIMIT),
        cost_estimate=LIGHT,
        name="add",
    )(in_vmem(arrived), in_vmem(kept), *before)


def per_device(features, adjacency, col_tiles, match_one, match_two):
    count, slots, width = adjacency.shape[:3]
    feat_count = features.shape[0]
    quarter = count // 4
    span = lax.axis_size("sub") * count
    blocks = adjacency.reshape(count, slots * width, width)
    work = Work(features, blocks, col_tiles.T, match_one, match_two, span)

    send = [(0, piece) for piece in range(quarter)]
    keep = [(1, piece) for piece in range(quarter)]
    first = work.run(leaving=send[:1])
    work.run(keys=send[:2], leaving=send[1:2], after=[first])
    lead = work.run(merges=send[:1])
    arrived = [swapped(lead, "blk")]
    parcel = work.run(merges=send[1:2], keys=send[2:], leaving=send[2:], apart=True, after=[lead])
    arrived.append(swapped(parcel, "blk"))
    parcel = work.run(merges=send[2:], after=[parcel, arrived[0]])
    arrived.append(swapped(parcel, "blk"))
    last = work.run(keys=keep, leaving=keep, apart=True, after=[parcel, arrived[1]])
    kept = work.run(merges=keep, after=[last])
    out = None
    piece = 0
    for part in arrived:
        out = added(piece, slots, feat_count, part, kept, out)
        piece += part.shape[0]
    return out[0].reshape(quarter, slots, width, width), out[1]


def solution(mesh):
    placed = (
        P(None, ("blk", "sub")),
        P(("blk", "sub"), None, None, None),
        P(("blk", "sub"), None),
        P(),
        P(),
    )
    return jax.shard_map(
        per_device,
        mesh=mesh,
        in_specs=placed,
        out_specs=(P(("blk", "sub"), None, None, None), P(None, ("blk", "sub"))),
        check_vma=False,
    )
```

```python
import functools

import jax
import jax.numpy as jnp
from jax import lax
from jax.experimental import pallas as pl
from jax.experimental.pallas import tpu as pltpu
from jax.sharding import PartitionSpec as P

HALF = 16
LIMIT = 48 * 2**20
LIGHT = pl.CostEstimate(flops=1, bytes_accessed=1, transcendentals=0)
VMEM = pl.BlockSpec(memory_space=pltpu.VMEM)
HBM = pl.BlockSpec(memory_space=pltpu.HBM)
ANY = pl.BlockSpec(memory_space=pl.ANY)


def swapped(value, axis):
    pairs = [(source, source ^ 1) for source in range(lax.axis_size(axis))]
    return lax.ppermute(value, axis, pairs)


def in_vmem(value):
    return pltpu.with_memory_space_constraint(value, pltpu.VMEM)


def in_hbm(value):
    return pltpu.with_memory_space_constraint(value, pltpu.HBM)


def split_by(value, size):
    if size & (size - 1) == 0:
        return value >> (size.bit_length() - 1), value & (size - 1)
    return value // size, value % size


def tile_at(phase, piece, partner):
    blk_bit = lax.axis_index("blk") & 1
    sub_bit = lax.axis_index("sub") & 1
    row_bit = blk_bit if phase == 1 else 1 - blk_bit
    return 4 * piece + 2 * row_bit + (1 - sub_bit if partner else sub_bit)


def start(source, target, sem):
    copy = pltpu.make_async_copy(source, target, sem)
    copy.start()
    return copy


def compose_maps(pick, span, count, cols, one_table, two_table, one_rows, two_rows, out):
    slots = cols.shape[0]
    lanes = lax.broadcasted_iota(jnp.int32, (1, one_table.shape[-1]), 1)

    def put(row, column_id):
        block, inside = split_by(column_id, span)
        pair_block, high_one = split_by(block, 2)
        sub, place = split_by(inside, count)
        sub_pair, high_two = split_by(sub, 2)
        pair = pair_block * span + inside
        group = pair_block * (span // 2) + sub_pair * count + place
        one_rows[pl.ds(row, 1), :] = jnp.where(high_one == 1, one_table[pl.ds(pair, 1), :], lanes)
        two_rows[pl.ds(row, 1), :] = jnp.where(high_two == 1, two_table[pl.ds(group, 1), :], lanes)

    one_rows[...] = jnp.zeros_like(one_rows)
    two_rows[...] = jnp.zeros_like(two_rows)
    tile = tile_at(*pick)
    for slot in range(slots):
        put(slot, cols[slot, tile])
    put(slots, lax.axis_index("blk") * span + lax.axis_index("sub") * count + tile)
    maps = jnp.take_along_axis(two_rows[...], one_rows[...], axis=1)
    out[...] = maps.astype(jnp.float32).astype(out.dtype)


def merge_tile(slots, width, own, other, own_side, other_side, put):
    along = lax.broadcasted_iota(jnp.int32, (width, width), 0).astype(jnp.float32)
    own_maps, other_maps = (x[:HALF].astype(jnp.float32) for x in (own_side, other_side))

    def hot(maps, row):
        return (maps[row : row + 1, :] == along).astype(jnp.bfloat16)

    def columns(row):
        return jnp.concatenate([hot(own_maps, row), hot(other_maps, row)], 1)

    def across(value, row):
        return lax.dot_general(
            value, columns(row), (((1,), (1,)), ((), ())), preferred_element_type=jnp.float32
        )

    def block_of(parts, slot):
        here, at = divmod(slot, slots // len(parts))
        return parts[here][at * width : (at + 1) * width, :]

    def moved(rows_hot, tile, pair):
        blocks = [block_of(tile, slot) for slot in (2 * pair, 2 * pair + 1)]
        value = jnp.dot(
            rows_hot, jnp.concatenate(blocks, 1), preferred_element_type=jnp.float32
        ).astype(jnp.bfloat16)
        return [value[:, :width], value[:, width:]]

    own_rows, other_rows = hot(own_maps, slots), hot(other_maps, slots)
    rows_done = []
    for pair in range(slots // 2):
        halves = moved(own_rows, own, pair), moved(other_rows, other, pair)
        rows_done += [jnp.concatenate(both, 1) for both in zip(*halves)]
    for slot, value in enumerate(rows_done):
        put(slot * width, across(value, slot).astype(jnp.bfloat16))
    feats = jnp.concatenate([own_side[HALF:], other_side[HALF:]], 1)
    put(slots * width, across(feats, slots).astype(jnp.bfloat16))


def work_kernel(plan, refs):
    rows = plan.rows
    copies, small = [], []
    if plan.picks:
        adjacency, features, cols, match_one, match_two = [refs[at] for at in plan.sources]
        cols_here, one_rows, two_rows, sems = [refs[at] for at in plan.scratch]
        one_table, two_table = [refs[at] for at in plan.tables]
        width = adjacency.shape[-1]
        small = [start(cols, cols_here, sems.at[2])]
        if plan.first:
            small += [
                start(match_one, one_table, sems.at[0]),
                start(match_two, two_table, sems.at[1]),
            ]
        sides = []
        for i, (pick, (mains, main_at, side, side_at)) in enumerate(zip(plan.picks, plan.targets)):
            tile = tile_at(*pick)
            lanes = pl.ds(pl.multiple_of(tile * width, width), width)
            sides.append(refs[side].at[pl.ds(side_at, HALF)])
            part = rows // len(mains)
            for at, main in enumerate(mains):
                copies.append(
                    start(
                        adjacency.at[tile, pl.ds(at * part, part)],
                        refs[main].at[pl.ds(main_at, part)],
                        sems.at[plan.sems[i] + at],
                    )
                )
            copies.append(
                start(
                    features.at[:, lanes],
                    refs[side].at[pl.ds(side_at + HALF, features.shape[0])],
                    sems.at[plan.sems[i] + len(mains)],
                )
            )
    for i, (own, other) in enumerate(plan.merges):
        tiles = [
            [refs[main].at[pl.ds(at, rows // len(mains))] for main in mains]
            for mains, at, _, _ in (own, other)
        ]
        ends = [refs[side][at : at + plan.depth - rows, :] for _, _, side, at in (own, other)]

        def put(row, value, base=i * plan.sum_depth):
            first, out = max(known for known in plan.outs if known[0] <= base + row)
            here = pl.ds(base + row - first, value.shape[0])
            refs[out][here, :] = value

        merge_tile(rows // plan.width, plan.width, *tiles, *ends, put)
    for copy in small:
        copy.wait()
    for i, pick in enumerate(plan.picks):
        compose_maps(
            pick, plan.span, plan.count, cols_here, one_table, two_table, one_rows, two_rows,
            sides[i],
        )
    for copy in copies:
        copy.wait()


class Plan:
    pass


class Work:
    def __init__(self, features, adjacency, cols, match_one, match_two, span):
        self.sources = [in_hbm(x) for x in (adjacency, features, cols, match_one, match_two)]
        self.tables = []
        self.span = span
        self.own, self.other = {}, {}

    def run(self, merges=(), keys=(), leaving=(), apart=(), after=(), cuts=()):
        adjacency, features, cols, match_one, match_two = self.sources
        rows, width = adjacency.shape[1:]
        plan = Plan()
        plan.rows, plan.depth = rows, rows + HALF + features.shape[0]
        plan.width, plan.sum_depth = width, rows + features.shape[0]
        plan.span, plan.count = self.span, cols.shape[1]
        plan.picks = [(*key, True) for key in leaving] + [(*key, False) for key in keys]
        ins, specs, shapes, scratch = [], [], [], []

        def take(value, spec):
            for place, known in enumerate(ins):
                if known is value:
                    return place
            ins.append(value)
            specs.append(spec)
            return len(ins) - 1

        plan.sources = [take(value, HBM) for value in self.sources] if plan.picks else []
        plan.first = not self.tables
        plan.tables = [take(value, VMEM) for value in self.tables] if plan.picks else []
        plan.merges = [
            [
                ([take(main, VMEM) for main in mains], at, take(side, VMEM), side_at)
                for mains, at, side, side_at in (self.own[key], self.other[key])
            ]
            for key in merges
        ]
        for value in after:
            take(value, ANY)

        def give(depth):
            shapes.append(pltpu.VMEM((depth, width), adjacency.dtype))
            return len(ins) + len(shapes) - 1

        edges = [0, *cuts, len(merges) * plan.sum_depth]
        sizes = [high - low for low, high in zip(edges, edges[1:])] if merges else []
        plan.outs = [(low, give(size)) for low, size in zip(edges, sizes)]
        extra = plan.depth - rows
        if apart:
            side = give(len(leaving) * extra)
            plan.targets = [
                ([give(rows // parts) for _ in range(parts)], 0, side, i * extra)
                for i, parts in enumerate(apart)
            ]
        else:
            mains = [give(plan.depth) for _ in leaving]
            plan.targets = [([main], 0, main, rows) for main in mains]
        if keys:
            pack = give(len(keys) * plan.depth)
            plan.targets += [
                ([pack], i * plan.depth, pack, i * plan.depth + rows) for i in range(len(keys))
            ]
        if plan.first:
            for table in (match_one, match_two):
                plan.tables.append(len(ins) + len(shapes))
                shapes.append(pltpu.VMEM(table.shape, table.dtype))
        plan.sems, total = [], 3
        for mains, _, _, _ in plan.targets:
            plan.sems.append(total)
            total += len(mains) + 1
        if plan.picks:
            scratch = [
                pltpu.SMEM(cols.shape, jnp.int32),
                pltpu.VMEM((HALF, width), jnp.int32),
                pltpu.VMEM((HALF, width), jnp.int32),
                pltpu.SemaphoreType.DMA((total,)),
            ]
        plan.scratch = [len(ins) + len(shapes) + i for i in range(len(scratch))]
        outs = pl.pallas_call(
            lambda *refs: work_kernel(plan, refs),
            out_shape=shapes,
            in_specs=specs,
            out_specs=[VMEM] * len(shapes),
            scratch_shapes=scratch,
            compiler_params=pltpu.CompilerParams(vmem_limit_bytes=LIMIT),
            cost_estimate=LIGHT,
            name="work",
        )(*ins)
        made = {len(ins) + i: value for i, value in enumerate(outs)}
        if plan.first:
            self.tables = [in_vmem(made[at]) for at in plan.tables]
        crossed = {}
        for pick, (mains, main_at, side, side_at) in zip(plan.picks, plan.targets):
            where = self.other if pick[2] else self.own
            for place in (*mains, side):
                if place not in crossed:
                    value = swapped(made[place], "sub") if pick[2] else made[place]
                    crossed[place] = in_vmem(value)
            where[pick[:2]] = ([crossed[main] for main in mains], main_at, crossed[side], side_at)
        return list(outs[: len(sizes)] if merges else outs)


def add_kernel(begin, depth, rows, arrived, kept, *rest):
    tiles_out, feats_out, total, sems = rest[-4:]
    width = arrived.shape[-1]
    end = begin + arrived.shape[0]
    copies = []
    for tile in range(begin // depth, -(-end // depth)):
        for low, high in ((0, rows), (rows, depth)):
            low, high = max(begin, tile * depth + low), min(end, tile * depth + high)
            if low >= high:
                continue
            here = slice(low - begin, high - begin)
            value = kept[low:high].astype(jnp.float32) + arrived[here].astype(jnp.float32)
            total[here] = value.astype(jnp.bfloat16)
            if high - tile * depth > rows:
                target = feats_out.at[:, pl.ds(tile * width, width)]
            else:
                target = tiles_out.at[tile, pl.ds(low - tile * depth, high - low)]
            source = total.at[pl.ds(low - begin, high - low)]
            copies.append(start(source, target, sems.at[len(copies)]))
    for copy in copies:
        copy.wait()


def added(begin, depth, rows, arrived, kept, before):
    size, width = arrived.shape
    quarter = kept.shape[0] // depth
    shapes = (
        jax.ShapeDtypeStruct((quarter, rows, width), jnp.bfloat16),
        jax.ShapeDtypeStruct((depth - rows, quarter * width), jnp.bfloat16),
    )
    return pl.pallas_call(
        functools.partial(add_kernel, begin, depth, rows),
        out_shape=shapes,
        in_specs=[VMEM, VMEM] + [HBM] * len(before),
        out_specs=(HBM, HBM),
        scratch_shapes=[
            pltpu.VMEM((size, width), jnp.bfloat16),
            pltpu.SemaphoreType.DMA((2 * quarter,)),
        ],
        input_output_aliases={2: 0, 3: 1} if before else {},
        compiler_params=pltpu.CompilerParams(vmem_limit_bytes=LIMIT),
        cost_estimate=LIGHT,
        name="add",
    )(in_vmem(arrived), in_vmem(kept), *before)


def per_device(features, adjacency, col_tiles, match_one, match_two):
    count, slots, width = adjacency.shape[:3]
    feat_count = features.shape[0]
    quarter = count // 4
    span = lax.axis_size("sub") * count
    blocks = adjacency.reshape(count, slots * width, width)
    work = Work(features, blocks, col_tiles.T, match_one, match_two, span)

    send = [(0, piece) for piece in range(quarter)]
    keep = [(1, piece) for piece in range(quarter)]
    rows = slots * width
    depth = rows + feat_count
    first = work.run(leaving=send[:1])
    work.run(keys=send[:1], leaving=send[1:2], after=first[:1])
    parcels = work.run(merges=send[:1])
    arrived = [swapped(parcels[0], "blk")]
    work.run(keys=send[1:], leaving=send[2:], apart=[1] * (quarter - 2), after=parcels)
    parcels = work.run(merges=send[1:2])
    arrived.append(swapped(parcels[0], "blk"))
    cut = (quarter - 3) * depth + slots // 2 * width
    parcels = work.run(merges=send[2:], after=parcels + arrived[:1], cuts=[cut])
    arrived += [swapped(parcel, "blk") for parcel in parcels]
    last = work.run(
        keys=keep, leaving=keep, apart=[1] * quarter, after=parcels[:1] + arrived[1:2]
    )
    kept = work.run(merges=keep, after=last[:1])[0]
    out = []
    begin = 0
    for part in arrived:
        out = added(begin, depth, rows, part, kept, out)
        begin += part.shape[0]
    return out[0].reshape(quarter, slots, width, width), out[1]


def solution(mesh):
    placed = (
        P(None, ("blk", "sub")),
        P(("blk", "sub"), None, None, None),
        P(("blk", "sub"), None),
        P(),
        P(),
    )
    return jax.shard_map(
        per_device,
        mesh=mesh,
        in_specs=placed,
        out_specs=(P(("blk", "sub"), None, None, None), P(None, ("blk", "sub"))),
        check_vma=False,
    )
```

```python
import functools

import jax
import jax.numpy as jnp
from jax import lax
from jax.experimental import pallas as pl
from jax.experimental.pallas import tpu as pltpu
from jax.sharding import PartitionSpec as P

HALF = 16
LIMIT = 48 * 2**20
LIGHT = pl.CostEstimate(flops=1, bytes_accessed=1, transcendentals=0)
VMEM = pl.BlockSpec(memory_space=pltpu.VMEM)
HBM = pl.BlockSpec(memory_space=pltpu.HBM)
ANY = pl.BlockSpec(memory_space=pl.ANY)


def swapped(value, axis):
    pairs = [(source, source ^ 1) for source in range(lax.axis_size(axis))]
    return lax.ppermute(value, axis, pairs)


def crossed_over(value):
    subs = lax.axis_size("sub")
    count = lax.axis_size("blk") * subs
    pairs = [(at, (at // subs ^ 1) * subs + (at % subs ^ 1)) for at in range(count)]
    return lax.ppermute(value, ("blk", "sub"), pairs)


def in_vmem(value):
    return pltpu.with_memory_space_constraint(value, pltpu.VMEM)


def in_hbm(value):
    return pltpu.with_memory_space_constraint(value, pltpu.HBM)


def split_by(value, size):
    if size & (size - 1) == 0:
        return value >> (size.bit_length() - 1), value & (size - 1)
    return value // size, value % size


def tile_at(phase, piece, partner):
    blk_bit = lax.axis_index("blk") & 1
    sub_bit = lax.axis_index("sub") & 1
    if phase == 0:
        blk_bit = 1 - blk_bit
    if partner == (phase == 1):
        sub_bit = 1 - sub_bit
    return 4 * piece + 2 * blk_bit + sub_bit


def start(source, target, sem):
    copy = pltpu.make_async_copy(source, target, sem)
    copy.start()
    return copy


def compose_maps(pick, span, count, cols, one_table, two_table, one_rows, two_rows, out):
    slots = cols.shape[0]
    lanes = lax.broadcasted_iota(jnp.int32, (1, one_table.shape[-1]), 1)

    def put(row, column_id):
        block, inside = split_by(column_id, span)
        pair_block, high_one = split_by(block, 2)
        sub, place = split_by(inside, count)
        sub_pair, high_two = split_by(sub, 2)
        pair = pair_block * span + inside
        group = pair_block * (span // 2) + sub_pair * count + place
        one_rows[pl.ds(row, 1), :] = jnp.where(high_one == 1, one_table[pl.ds(pair, 1), :], lanes)
        two_rows[pl.ds(row, 1), :] = jnp.where(high_two == 1, two_table[pl.ds(group, 1), :], lanes)

    one_rows[...] = jnp.zeros_like(one_rows)
    two_rows[...] = jnp.zeros_like(two_rows)
    tile = tile_at(*pick)
    for slot in range(slots):
        put(slot, cols[slot, tile])
    put(slots, lax.axis_index("blk") * span + lax.axis_index("sub") * count + tile)
    maps = jnp.take_along_axis(two_rows[...], one_rows[...], axis=1)
    out[...] = maps.astype(jnp.float32).astype(out.dtype)


def merge_tile(slots, width, own, other, own_side, other_side, put):
    along = lax.broadcasted_iota(jnp.int32, (width, width), 0).astype(jnp.float32)
    own_maps, other_maps = (x[:HALF].astype(jnp.float32) for x in (own_side, other_side))

    def hot(maps, row):
        return (maps[row : row + 1, :] == along).astype(jnp.bfloat16)

    def columns(row):
        return jnp.concatenate([hot(own_maps, row), hot(other_maps, row)], 1)

    def across(value, row):
        return lax.dot_general(
            value, columns(row), (((1,), (1,)), ((), ())), preferred_element_type=jnp.float32
        )

    def block_of(parts, slot):
        here, at = divmod(slot, slots // len(parts))
        return parts[here][at * width : (at + 1) * width, :]

    def moved(rows_hot, tile, pair):
        blocks = [block_of(tile, slot) for slot in (2 * pair, 2 * pair + 1)]
        value = jnp.dot(
            rows_hot, jnp.concatenate(blocks, 1), preferred_element_type=jnp.float32
        ).astype(jnp.bfloat16)
        return [value[:, :width], value[:, width:]]

    own_rows, other_rows = hot(own_maps, slots), hot(other_maps, slots)
    rows_done = []
    for pair in range(slots // 2):
        halves = moved(own_rows, own, pair), moved(other_rows, other, pair)
        rows_done += [jnp.concatenate(both, 1) for both in zip(*halves)]
    for slot, value in enumerate(rows_done):
        put(slot * width, across(value, slot).astype(jnp.bfloat16))
    feats = jnp.concatenate([own_side[HALF:], other_side[HALF:]], 1)
    put(slots * width, across(feats, slots).astype(jnp.bfloat16))


def work_kernel(plan, refs):
    rows = plan.rows
    copies, small = [], []
    if plan.picks:
        adjacency, features, cols, match_one, match_two = [refs[at] for at in plan.sources]
        cols_here, one_rows, two_rows, sems = [refs[at] for at in plan.scratch]
        one_table, two_table = [refs[at] for at in plan.tables]
        width = adjacency.shape[-1]
        small = [start(cols, cols_here, sems.at[2])]
        if plan.first:
            small += [
                start(match_one, one_table, sems.at[0]),
                start(match_two, two_table, sems.at[1]),
            ]
        sides = []
        for i, (pick, (mains, main_at, side, side_at)) in enumerate(zip(plan.picks, plan.targets)):
            tile = tile_at(*pick)
            lanes = pl.ds(pl.multiple_of(tile * width, width), width)
            sides.append(refs[side].at[pl.ds(side_at, HALF)])
            part = rows // len(mains)
            for at, main in enumerate(mains):
                copies.append(
                    start(
                        adjacency.at[tile, pl.ds(at * part, part)],
                        refs[main].at[pl.ds(main_at, part)],
                        sems.at[plan.sems[i] + at],
                    )
                )
            copies.append(
                start(
                    features.at[:, lanes],
                    refs[side].at[pl.ds(side_at + HALF, features.shape[0])],
                    sems.at[plan.sems[i] + len(mains)],
                )
            )
    for i, (own, other) in enumerate(plan.merges):
        tiles = [
            [refs[main].at[pl.ds(at, rows // len(mains))] for main in mains]
            for mains, at, _, _ in (own, other)
        ]
        ends = [refs[side][at : at + plan.depth - rows, :] for _, _, side, at in (own, other)]

        def put(row, value, base=i * plan.sum_depth):
            first, out = max(known for known in plan.outs if known[0] <= base + row)
            here = pl.ds(base + row - first, value.shape[0])
            refs[out][here, :] = value

        merge_tile(rows // plan.width, plan.width, *tiles, *ends, put)
    for copy in small:
        copy.wait()
    for i, pick in enumerate(plan.picks):
        compose_maps(
            pick, plan.span, plan.count, cols_here, one_table, two_table, one_rows, two_rows,
            sides[i],
        )
    for copy in copies:
        copy.wait()


class Plan:
    pass


class Work:
    def __init__(self, features, adjacency, cols, match_one, match_two, span):
        self.sources = [in_hbm(x) for x in (adjacency, features, cols, match_one, match_two)]
        self.tables = []
        self.span = span
        self.own, self.other = {}, {}

    def run(self, merges=(), keys=(), leaving=(), apart=(), after=(), cuts=()):
        adjacency, features, cols, match_one, match_two = self.sources
        rows, width = adjacency.shape[1:]
        plan = Plan()
        plan.rows, plan.depth = rows, rows + HALF + features.shape[0]
        plan.width, plan.sum_depth = width, rows + features.shape[0]
        plan.span, plan.count = self.span, cols.shape[1]
        plan.picks = [(*key, True) for key in leaving] + [(*key, False) for key in keys]
        ins, specs, shapes, scratch = [], [], [], []

        def take(value, spec):
            for place, known in enumerate(ins):
                if known is value:
                    return place
            ins.append(value)
            specs.append(spec)
            return len(ins) - 1

        plan.sources = [take(value, HBM) for value in self.sources] if plan.picks else []
        plan.first = not self.tables
        plan.tables = [take(value, VMEM) for value in self.tables] if plan.picks else []
        plan.merges = [
            [
                ([take(main, VMEM) for main in mains], at, take(side, VMEM), side_at)
                for mains, at, side, side_at in (self.own[key], self.other[key])
            ]
            for key in merges
        ]
        for value in after:
            take(value, ANY)

        def give(depth):
            shapes.append(pltpu.VMEM((depth, width), adjacency.dtype))
            return len(ins) + len(shapes) - 1

        edges = [0, *cuts, len(merges) * plan.sum_depth]
        sizes = [high - low for low, high in zip(edges, edges[1:])] if merges else []
        plan.outs = [(low, give(size)) for low, size in zip(edges, sizes)]
        extra = plan.depth - rows
        if apart:
            side = give(len(leaving) * extra)
            plan.targets = [
                ([give(rows // parts) for _ in range(parts)], 0, side, i * extra)
                for i, parts in enumerate(apart)
            ]
        else:
            mains = [give(plan.depth) for _ in leaving]
            plan.targets = [([main], 0, main, rows) for main in mains]
        if keys:
            pack = give(len(keys) * plan.depth)
            plan.targets += [
                ([pack], i * plan.depth, pack, i * plan.depth + rows) for i in range(len(keys))
            ]
        if plan.first:
            for table in (match_one, match_two):
                plan.tables.append(len(ins) + len(shapes))
                shapes.append(pltpu.VMEM(table.shape, table.dtype))
        plan.sems, total = [], 3
        for mains, _, _, _ in plan.targets:
            plan.sems.append(total)
            total += len(mains) + 1
        if plan.picks:
            scratch = [
                pltpu.SMEM(cols.shape, jnp.int32),
                pltpu.VMEM((HALF, width), jnp.int32),
                pltpu.VMEM((HALF, width), jnp.int32),
                pltpu.SemaphoreType.DMA((total,)),
            ]
        plan.scratch = [len(ins) + len(shapes) + i for i in range(len(scratch))]
        outs = pl.pallas_call(
            lambda *refs: work_kernel(plan, refs),
            out_shape=shapes,
            in_specs=specs,
            out_specs=[VMEM] * len(shapes),
            scratch_shapes=scratch,
            compiler_params=pltpu.CompilerParams(vmem_limit_bytes=LIMIT),
            cost_estimate=LIGHT,
            name="work",
        )(*ins)
        made = {len(ins) + i: value for i, value in enumerate(outs)}
        if plan.first:
            self.tables = [in_vmem(made[at]) for at in plan.tables]
        crossed = {}
        for pick, (mains, main_at, side, side_at) in zip(plan.picks, plan.targets):
            where = self.other if pick[2] else self.own
            for place in (*mains, side):
                if place not in crossed:
                    value = swapped(made[place], "sub") if pick[2] else made[place]
                    crossed[place] = in_vmem(value)
            where[pick[:2]] = ([crossed[main] for main in mains], main_at, crossed[side], side_at)
        return list(outs[: len(sizes)] if merges else outs)


def add_kernel(begin, depth, rows, arrived, kept, *rest):
    tiles_out, feats_out, total, sems = rest[-4:]
    width = arrived.shape[-1]
    end = begin + arrived.shape[0]
    copies = []
    for tile in range(begin // depth, -(-end // depth)):
        for low, high in ((0, rows), (rows, depth)):
            low, high = max(begin, tile * depth + low), min(end, tile * depth + high)
            if low >= high:
                continue
            here = slice(low - begin, high - begin)
            value = kept[low:high].astype(jnp.float32) + arrived[here].astype(jnp.float32)
            total[here] = value.astype(jnp.bfloat16)
            if high - tile * depth > rows:
                target = feats_out.at[:, pl.ds(tile * width, width)]
            else:
                target = tiles_out.at[tile, pl.ds(low - tile * depth, high - low)]
            source = total.at[pl.ds(low - begin, high - low)]
            copies.append(start(source, target, sems.at[len(copies)]))
    for copy in copies:
        copy.wait()


def added(begin, depth, rows, arrived, kept, before):
    size, width = arrived.shape
    quarter = kept.shape[0] // depth
    shapes = (
        jax.ShapeDtypeStruct((quarter, rows, width), jnp.bfloat16),
        jax.ShapeDtypeStruct((depth - rows, quarter * width), jnp.bfloat16),
    )
    return pl.pallas_call(
        functools.partial(add_kernel, begin, depth, rows),
        out_shape=shapes,
        in_specs=[VMEM, VMEM] + [HBM] * len(before),
        out_specs=(HBM, HBM),
        scratch_shapes=[
            pltpu.VMEM((size, width), jnp.bfloat16),
            pltpu.SemaphoreType.DMA((2 * quarter,)),
        ],
        input_output_aliases={2: 0, 3: 1} if before else {},
        compiler_params=pltpu.CompilerParams(vmem_limit_bytes=LIMIT),
        cost_estimate=LIGHT,
        name="add",
    )(in_vmem(arrived), in_vmem(kept), *before)


def per_device(features, adjacency, col_tiles, match_one, match_two):
    count, slots, width = adjacency.shape[:3]
    feat_count = features.shape[0]
    quarter = count // 4
    span = lax.axis_size("sub") * count
    blocks = adjacency.reshape(count, slots * width, width)
    work = Work(features, blocks, col_tiles.T, match_one, match_two, span)

    send = [(0, piece) for piece in range(quarter)]
    keep = [(1, piece) for piece in range(quarter)]
    rows = slots * width
    depth = rows + feat_count
    first = work.run(leaving=send[:1])
    work.run(keys=send[:1], leaving=send[1:2], after=first[:1])
    parcels = work.run(merges=send[:1])
    arrived = [crossed_over(parcels[0])]
    work.run(keys=send[1:], leaving=send[2:], apart=[1] * (quarter - 2), after=parcels)
    parcels = work.run(merges=send[1:2])
    arrived.append(crossed_over(parcels[0]))
    cut = (quarter - 3) * depth + slots // 2 * width
    parcels = work.run(merges=send[2:], after=parcels + arrived[:1], cuts=[cut])
    arrived += [crossed_over(parcel) for parcel in parcels]
    last = work.run(
        keys=keep, leaving=keep, apart=[1] * quarter, after=parcels[:1] + arrived[1:2]
    )
    kept = work.run(merges=keep, after=last[:1])[0]
    out = []
    begin = 0
    for part in arrived:
        out = added(begin, depth, rows, part, kept, out)
        begin += part.shape[0]
    return out[0].reshape(quarter, slots, width, width), out[1]


def solution(mesh):
    placed = (
        P(None, ("blk", "sub")),
        P(("blk", "sub"), None, None, None),
        P(("blk", "sub"), None),
        P(),
        P(),
    )
    return jax.shard_map(
        per_device,
        mesh=mesh,
        in_specs=placed,
        out_specs=(P(("blk", "sub"), None, None, None), P(None, ("blk", "sub"))),
        check_vma=False,
    )
```

```python
import functools

import jax
import jax.numpy as jnp
from jax import lax
from jax.experimental import pallas as pl
from jax.experimental.pallas import tpu as pltpu
from jax.sharding import PartitionSpec as P

HALF = 16
LIMIT = 48 * 2**20
LIGHT = pl.CostEstimate(flops=1, bytes_accessed=1, transcendentals=0)
VMEM = pl.BlockSpec(memory_space=pltpu.VMEM)
HBM = pl.BlockSpec(memory_space=pltpu.HBM)
ANY = pl.BlockSpec(memory_space=pl.ANY)


def swapped(value, axis):
    pairs = [(source, source ^ 1) for source in range(lax.axis_size(axis))]
    return lax.ppermute(value, axis, pairs)


def crossed_over(value):
    subs = lax.axis_size("sub")
    count = lax.axis_size("blk") * subs
    pairs = [(at, (at // subs ^ 1) * subs + (at % subs ^ 1)) for at in range(count)]
    return lax.ppermute(value, ("blk", "sub"), pairs)


def in_vmem(value):
    return pltpu.with_memory_space_constraint(value, pltpu.VMEM)


def in_hbm(value):
    return pltpu.with_memory_space_constraint(value, pltpu.HBM)


def split_by(value, size):
    if size & (size - 1) == 0:
        return value >> (size.bit_length() - 1), value & (size - 1)
    return value // size, value % size


def tile_at(phase, piece, partner):
    blk_bit = lax.axis_index("blk") & 1
    sub_bit = lax.axis_index("sub") & 1
    if phase == 0:
        blk_bit = 1 - blk_bit
    if partner == (phase == 1):
        sub_bit = 1 - sub_bit
    return 4 * piece + 2 * blk_bit + sub_bit


def start(source, target, sem):
    copy = pltpu.make_async_copy(source, target, sem)
    copy.start()
    return copy


def compose_maps(pick, span, count, cols, one_table, two_table, one_rows, two_rows, out):
    slots = cols.shape[0]
    lanes = lax.broadcasted_iota(jnp.int32, (1, one_table.shape[-1]), 1)

    def put(row, column_id):
        block, inside = split_by(column_id, span)
        pair_block, high_one = split_by(block, 2)
        sub, place = split_by(inside, count)
        sub_pair, high_two = split_by(sub, 2)
        pair = pair_block * span + inside
        group = pair_block * (span // 2) + sub_pair * count + place
        one_rows[pl.ds(row, 1), :] = jnp.where(high_one == 1, one_table[pl.ds(pair, 1), :], lanes)
        two_rows[pl.ds(row, 1), :] = jnp.where(high_two == 1, two_table[pl.ds(group, 1), :], lanes)

    one_rows[...] = jnp.zeros_like(one_rows)
    two_rows[...] = jnp.zeros_like(two_rows)
    tile = tile_at(*pick)
    for slot in range(slots):
        put(slot, cols[slot, tile])
    put(slots, lax.axis_index("blk") * span + lax.axis_index("sub") * count + tile)
    maps = jnp.take_along_axis(two_rows[...], one_rows[...], axis=1)
    out[...] = maps.astype(jnp.float32).astype(out.dtype)


def merge_tile(slots, width, own, other, own_side, other_side, put):
    along = lax.broadcasted_iota(jnp.int32, (width, width), 0).astype(jnp.float32)
    own_maps, other_maps = (x[:HALF].astype(jnp.float32) for x in (own_side, other_side))

    def hot(maps, row):
        return (maps[row : row + 1, :] == along).astype(jnp.bfloat16)

    def columns(row):
        return jnp.concatenate([hot(own_maps, row), hot(other_maps, row)], 1)

    def across(value, row):
        return lax.dot_general(
            value, columns(row), (((1,), (1,)), ((), ())), preferred_element_type=jnp.float32
        )

    def block_of(parts, slot):
        here, at = divmod(slot, slots // len(parts))
        return parts[here][at * width : (at + 1) * width, :]

    def moved(rows_hot, tile, pair):
        blocks = [block_of(tile, slot) for slot in (2 * pair, 2 * pair + 1)]
        value = jnp.dot(
            rows_hot, jnp.concatenate(blocks, 1), preferred_element_type=jnp.float32
        ).astype(jnp.bfloat16)
        return [value[:, :width], value[:, width:]]

    own_rows, other_rows = hot(own_maps, slots), hot(other_maps, slots)
    rows_done = []
    for pair in range(slots // 2):
        halves = moved(own_rows, own, pair), moved(other_rows, other, pair)
        rows_done += [jnp.concatenate(both, 1) for both in zip(*halves)]
    for slot, value in enumerate(rows_done):
        put(slot * width, across(value, slot).astype(jnp.bfloat16))
    feats = jnp.concatenate([own_side[HALF:], other_side[HALF:]], 1)
    put(slots * width, across(feats, slots).astype(jnp.bfloat16))


def work_kernel(plan, refs):
    rows = plan.rows
    copies, small = [], []
    if plan.picks:
        adjacency, features, cols, match_one, match_two = [refs[at] for at in plan.sources]
        cols_here, one_rows, two_rows, sems = [refs[at] for at in plan.scratch]
        one_table, two_table = [refs[at] for at in plan.tables]
        width = adjacency.shape[-1]
        small = [start(cols, cols_here, sems.at[2])]
        if plan.first:
            small += [
                start(match_one, one_table, sems.at[0]),
                start(match_two, two_table, sems.at[1]),
            ]
        sides = []
        for i, (pick, (mains, main_at, side, side_at)) in enumerate(zip(plan.picks, plan.targets)):
            tile = tile_at(*pick)
            lanes = pl.ds(pl.multiple_of(tile * width, width), width)
            sides.append(refs[side].at[pl.ds(side_at, HALF)])
            part = rows // len(mains)
            for at, main in enumerate(mains):
                copies.append(
                    start(
                        adjacency.at[tile, pl.ds(at * part, part)],
                        refs[main].at[pl.ds(main_at, part)],
                        sems.at[plan.sems[i] + at],
                    )
                )
            copies.append(
                start(
                    features.at[:, lanes],
                    refs[side].at[pl.ds(side_at + HALF, features.shape[0])],
                    sems.at[plan.sems[i] + len(mains)],
                )
            )
    for i, (own, other) in enumerate(plan.merges):
        tiles = [
            [refs[main].at[pl.ds(at, rows // len(mains))] for main in mains]
            for mains, at, _, _ in (own, other)
        ]
        ends = [refs[side][at : at + plan.depth - rows, :] for _, _, side, at in (own, other)]

        def put(row, value, base=i * plan.sum_depth):
            first, out = max(known for known in plan.outs if known[0] <= base + row)
            here = pl.ds(base + row - first, value.shape[0])
            refs[out][here, :] = value

        merge_tile(rows // plan.width, plan.width, *tiles, *ends, put)
    for copy in small:
        copy.wait()
    for i, pick in enumerate(plan.picks):
        compose_maps(
            pick, plan.span, plan.count, cols_here, one_table, two_table, one_rows, two_rows,
            sides[i],
        )
    for copy in copies:
        copy.wait()


class Plan:
    pass


class Work:
    def __init__(self, features, adjacency, cols, match_one, match_two, span):
        self.sources = [in_hbm(x) for x in (adjacency, features, cols, match_one, match_two)]
        self.tables = []
        self.span = span
        self.own, self.other = {}, {}

    def run(self, merges=(), keys=(), leaving=(), apart=(), after=(), cuts=()):
        adjacency, features, cols, match_one, match_two = self.sources
        rows, width = adjacency.shape[1:]
        plan = Plan()
        plan.rows, plan.depth = rows, rows + HALF + features.shape[0]
        plan.width, plan.sum_depth = width, rows + features.shape[0]
        plan.span, plan.count = self.span, cols.shape[1]
        plan.picks = [(*key, True) for key in leaving] + [(*key, False) for key in keys]
        ins, specs, shapes, scratch = [], [], [], []

        def take(value, spec):
            for place, known in enumerate(ins):
                if known is value:
                    return place
            ins.append(value)
            specs.append(spec)
            return len(ins) - 1

        plan.sources = [take(value, HBM) for value in self.sources] if plan.picks else []
        plan.first = not self.tables
        plan.tables = [take(value, VMEM) for value in self.tables] if plan.picks else []
        plan.merges = [
            [
                ([take(main, VMEM) for main in mains], at, take(side, VMEM), side_at)
                for mains, at, side, side_at in (self.own[key], self.other[key])
            ]
            for key in merges
        ]
        for value in after:
            take(value, ANY)

        def give(depth):
            shapes.append(pltpu.VMEM((depth, width), adjacency.dtype))
            return len(ins) + len(shapes) - 1

        edges = [0, *cuts, len(merges) * plan.sum_depth]
        sizes = [high - low for low, high in zip(edges, edges[1:])] if merges else []
        plan.outs = [(low, give(size)) for low, size in zip(edges, sizes)]
        extra = plan.depth - rows
        if apart:
            side = give(len(leaving) * extra)
            plan.targets = [
                ([give(rows // parts) for _ in range(parts)], 0, side, i * extra)
                for i, parts in enumerate(apart)
            ]
        else:
            mains = [give(plan.depth) for _ in leaving]
            plan.targets = [([main], 0, main, rows) for main in mains]
        if keys:
            pack = give(len(keys) * plan.depth)
            plan.targets += [
                ([pack], i * plan.depth, pack, i * plan.depth + rows) for i in range(len(keys))
            ]
        if plan.first:
            for table in (match_one, match_two):
                plan.tables.append(len(ins) + len(shapes))
                shapes.append(pltpu.VMEM(table.shape, table.dtype))
        plan.sems, total = [], 3
        for mains, _, _, _ in plan.targets:
            plan.sems.append(total)
            total += len(mains) + 1
        if plan.picks:
            scratch = [
                pltpu.SMEM(cols.shape, jnp.int32),
                pltpu.VMEM((HALF, width), jnp.int32),
                pltpu.VMEM((HALF, width), jnp.int32),
                pltpu.SemaphoreType.DMA((total,)),
            ]
        plan.scratch = [len(ins) + len(shapes) + i for i in range(len(scratch))]
        outs = pl.pallas_call(
            lambda *refs: work_kernel(plan, refs),
            out_shape=shapes,
            in_specs=specs,
            out_specs=[VMEM] * len(shapes),
            scratch_shapes=scratch,
            compiler_params=pltpu.CompilerParams(vmem_limit_bytes=LIMIT),
            cost_estimate=LIGHT,
            name="work",
        )(*ins)
        made = {len(ins) + i: value for i, value in enumerate(outs)}
        if plan.first:
            self.tables = [in_vmem(made[at]) for at in plan.tables]
        crossed = {}
        for pick, (mains, main_at, side, side_at) in zip(plan.picks, plan.targets):
            where = self.other if pick[2] else self.own
            for place in (*mains, side):
                if place not in crossed:
                    value = swapped(made[place], "sub") if pick[2] else made[place]
                    crossed[place] = in_vmem(value)
            where[pick[:2]] = ([crossed[main] for main in mains], main_at, crossed[side], side_at)
        return list(outs[: len(sizes)] if merges else outs)


def add_kernel(begin, depth, rows, arrived, kept, *rest):
    tiles_out, feats_out, total, sems = rest[-4:]
    width = arrived.shape[-1]
    end = begin + arrived.shape[0]
    copies = []
    for tile in range(begin // depth, -(-end // depth)):
        for low, high in ((0, rows), (rows, depth)):
            low, high = max(begin, tile * depth + low), min(end, tile * depth + high)
            if low >= high:
                continue
            here = slice(low - begin, high - begin)
            value = kept[low:high].astype(jnp.float32) + arrived[here].astype(jnp.float32)
            total[here] = value.astype(jnp.bfloat16)
            if high - tile * depth > rows:
                target = feats_out.at[:, pl.ds(tile * width, width)]
            else:
                target = tiles_out.at[tile, pl.ds(low - tile * depth, high - low)]
            source = total.at[pl.ds(low - begin, high - low)]
            copies.append(start(source, target, sems.at[len(copies)]))
    for copy in copies:
        copy.wait()


def added(begin, depth, rows, arrived, kept, before):
    size, width = arrived.shape
    quarter = kept.shape[0] // depth
    shapes = (
        jax.ShapeDtypeStruct((quarter, rows, width), jnp.bfloat16),
        jax.ShapeDtypeStruct((depth - rows, quarter * width), jnp.bfloat16),
    )
    return pl.pallas_call(
        functools.partial(add_kernel, begin, depth, rows),
        out_shape=shapes,
        in_specs=[VMEM, VMEM] + [HBM] * len(before),
        out_specs=(HBM, HBM),
        scratch_shapes=[
            pltpu.VMEM((size, width), jnp.bfloat16),
            pltpu.SemaphoreType.DMA((2 * quarter,)),
        ],
        input_output_aliases={2: 0, 3: 1} if before else {},
        compiler_params=pltpu.CompilerParams(vmem_limit_bytes=LIMIT),
        cost_estimate=LIGHT,
        name="add",
    )(in_vmem(arrived), in_vmem(kept), *before)


def per_device(features, adjacency, col_tiles, match_one, match_two):
    count, slots, width = adjacency.shape[:3]
    feat_count = features.shape[0]
    quarter = count // 4
    span = lax.axis_size("sub") * count
    blocks = adjacency.reshape(count, slots * width, width)
    work = Work(features, blocks, col_tiles.T, match_one, match_two, span)

    send = [(0, piece) for piece in range(quarter)]
    keep = [(1, piece) for piece in range(quarter)]
    rows = slots * width
    depth = rows + feat_count
    first = work.run(leaving=send[:2])
    work.run(keys=send[:1], after=first[:1])
    parcels = work.run(merges=send[:1])
    arrived = [crossed_over(parcels[0])]
    work.run(keys=send[1:], leaving=send[2:], apart=[1] * (quarter - 2), after=parcels)
    parcels = work.run(merges=send[1:2])
    arrived.append(crossed_over(parcels[0]))
    cut = (quarter - 3) * depth + slots // 2 * width
    parcels = work.run(merges=send[2:], after=parcels + arrived[:1], cuts=[cut])
    arrived += [crossed_over(parcel) for parcel in parcels]
    last = work.run(
        keys=keep, leaving=keep, apart=[1] * quarter, after=parcels[:1] + arrived[1:2]
    )
    kept = work.run(merges=keep, after=last[:1])[0]
    out = []
    begin = 0
    for part in arrived:
        out = added(begin, depth, rows, part, kept, out)
        begin += part.shape[0]
    return out[0].reshape(quarter, slots, width, width), out[1]


def solution(mesh):
    placed = (
        P(None, ("blk", "sub")),
        P(("blk", "sub"), None, None, None),
        P(("blk", "sub"), None),
        P(),
        P(),
    )
    return jax.shard_map(
        per_device,
        mesh=mesh,
        in_specs=placed,
        out_specs=(P(("blk", "sub"), None, None, None), P(None, ("blk", "sub"))),
        check_vma=False,
    )
```

```python
import functools

import jax
import jax.numpy as jnp
from jax import lax
from jax.experimental import pallas as pl
from jax.experimental.pallas import tpu as pltpu
from jax.sharding import PartitionSpec as P

HALF = 16
LIMIT = 48 * 2**20
LIGHT = pl.CostEstimate(flops=1, bytes_accessed=1, transcendentals=0)
VMEM = pl.BlockSpec(memory_space=pltpu.VMEM)
HBM = pl.BlockSpec(memory_space=pltpu.HBM)
ANY = pl.BlockSpec(memory_space=pl.ANY)


def swapped(value, axis):
    pairs = [(source, source ^ 1) for source in range(lax.axis_size(axis))]
    return lax.ppermute(value, axis, pairs)


def crossed_over(value):
    subs = lax.axis_size("sub")
    count = lax.axis_size("blk") * subs
    pairs = [(at, (at // subs ^ 1) * subs + (at % subs ^ 1)) for at in range(count)]
    return lax.ppermute(value, ("blk", "sub"), pairs)


def in_vmem(value):
    return pltpu.with_memory_space_constraint(value, pltpu.VMEM)


def in_hbm(value):
    return pltpu.with_memory_space_constraint(value, pltpu.HBM)


def split_by(value, size):
    if size & (size - 1) == 0:
        return value >> (size.bit_length() - 1), value & (size - 1)
    return value // size, value % size


def pieces_of(slots, count):
    edges = [slots * at // count for at in range(count + 1)]
    return list(zip(edges, edges[1:]))


def tile_at(phase, piece, partner):
    blk_bit = lax.axis_index("blk") & 1
    sub_bit = lax.axis_index("sub") & 1
    if phase == 0:
        blk_bit = 1 - blk_bit
    if partner == (phase == 1):
        sub_bit = 1 - sub_bit
    return 4 * piece + 2 * blk_bit + sub_bit


def start(source, target, sem):
    copy = pltpu.make_async_copy(source, target, sem)
    copy.start()
    return copy


def compose_maps(pick, span, count, cols, one_table, two_table, one_rows, two_rows, out):
    slots = cols.shape[0]
    lanes = lax.broadcasted_iota(jnp.int32, (1, one_table.shape[-1]), 1)

    def put(row, column_id):
        block, inside = split_by(column_id, span)
        pair_block, high_one = split_by(block, 2)
        sub, place = split_by(inside, count)
        sub_pair, high_two = split_by(sub, 2)
        pair = pair_block * span + inside
        group = pair_block * (span // 2) + sub_pair * count + place
        one_rows[pl.ds(row, 1), :] = jnp.where(high_one == 1, one_table[pl.ds(pair, 1), :], lanes)
        two_rows[pl.ds(row, 1), :] = jnp.where(high_two == 1, two_table[pl.ds(group, 1), :], lanes)

    one_rows[...] = jnp.zeros_like(one_rows)
    two_rows[...] = jnp.zeros_like(two_rows)
    tile = tile_at(*pick)
    for slot in range(slots):
        put(slot, cols[slot, tile])
    put(slots, lax.axis_index("blk") * span + lax.axis_index("sub") * count + tile)
    maps = jnp.take_along_axis(two_rows[...], one_rows[...], axis=1)
    out[...] = maps.astype(jnp.float32).astype(out.dtype)


def merge_tile(slots, width, own, other, own_side, other_side, wanted, put):
    along = lax.broadcasted_iota(jnp.int32, (width, width), 0).astype(jnp.float32)
    own_maps, other_maps = (x[:HALF].astype(jnp.float32) for x in (own_side, other_side))

    def hot(maps, row):
        return (maps[row : row + 1, :] == along).astype(jnp.bfloat16)

    def columns(row):
        return jnp.concatenate([hot(own_maps, row), hot(other_maps, row)], 1)

    def across(value, row):
        return lax.dot_general(
            value, columns(row), (((1,), (1,)), ((), ())), preferred_element_type=jnp.float32
        )

    def block_of(parts, slot):
        for part, (first, end) in zip(parts, pieces_of(slots, len(parts))):
            if first <= slot < end:
                return part[(slot - first) * width : (slot - first + 1) * width, :]

    def moved(rows_hot, tile, pair):
        blocks = [block_of(tile, slot) for slot in (2 * pair, 2 * pair + 1)]
        value = jnp.dot(
            rows_hot, jnp.concatenate(blocks, 1), preferred_element_type=jnp.float32
        ).astype(jnp.bfloat16)
        return [value[:, :width], value[:, width:]]

    own_rows, other_rows = hot(own_maps, slots), hot(other_maps, slots)
    rows_done = {}
    for pair in range(slots // 2):
        if wanted(2 * pair * width):
            halves = moved(own_rows, own, pair), moved(other_rows, other, pair)
            for at, both in enumerate(zip(*halves)):
                rows_done[2 * pair + at] = jnp.concatenate(both, 1)
    for slot, value in rows_done.items():
        put(slot * width, across(value, slot).astype(jnp.bfloat16))
    if wanted(slots * width):
        feats = jnp.concatenate([own_side[HALF:], other_side[HALF:]], 1)
        put(slots * width, across(feats, slots).astype(jnp.bfloat16))


def work_kernel(plan, refs):
    rows = plan.rows
    copies, small = [], []
    if plan.picks:
        adjacency, features, cols, match_one, match_two = [refs[at] for at in plan.sources]
        cols_here, one_rows, two_rows, sems = [refs[at] for at in plan.scratch]
        one_table, two_table = [refs[at] for at in plan.tables]
        width = adjacency.shape[-1]
        small = [start(cols, cols_here, sems.at[2])]
        if plan.first:
            small += [
                start(match_one, one_table, sems.at[0]),
                start(match_two, two_table, sems.at[1]),
            ]
        sides = []
        for i, (pick, (mains, main_at, side, side_at)) in enumerate(zip(plan.picks, plan.targets)):
            tile = tile_at(*pick)
            lanes = pl.ds(pl.multiple_of(tile * width, width), width)
            sides.append(refs[side].at[pl.ds(side_at, HALF)])
            for at, (first, end) in enumerate(pieces_of(rows // width, len(mains))):
                size = (end - first) * width
                copies.append(
                    start(
                        adjacency.at[tile, pl.ds(first * width, size)],
                        refs[mains[at]].at[pl.ds(main_at, size)],
                        sems.at[plan.sems[i] + at],
                    )
                )
            copies.append(
                start(
                    features.at[:, lanes],
                    refs[side].at[pl.ds(side_at + HALF, features.shape[0])],
                    sems.at[plan.sems[i] + len(mains)],
                )
            )
    for i, (own, other) in enumerate(plan.merges):
        tiles = [
            [
                None if main is None else refs[main].at[pl.ds(at, (end - first) * plan.width)]
                for main, (first, end) in zip(mains, pieces_of(rows // plan.width, len(mains)))
            ]
            for mains, at, _, _ in (own, other)
        ]
        ends = [refs[side][at : at + plan.depth - rows, :] for _, _, side, at in (own, other)]

        def wanted(row, base=i * plan.sum_depth):
            return plan.place(base + row) is not None

        def put(row, value, base=i * plan.sum_depth):
            out, at = plan.place(base + row)
            refs[out][pl.ds(at, value.shape[0]), :] = value

        merge_tile(rows // plan.width, plan.width, *tiles, *ends, wanted, put)
    for copy in small:
        copy.wait()
    for i, pick in enumerate(plan.picks):
        compose_maps(
            pick, plan.span, plan.count, cols_here, one_table, two_table, one_rows, two_rows,
            sides[i],
        )
    for copy in copies:
        copy.wait()


class Plan:
    def place(self, row):
        for out, segments in self.outs:
            at = 0
            for first, size in segments:
                if first <= row < first + size:
                    return out, at + row - first
                at += size
        return None


class Work:
    def __init__(self, features, adjacency, cols, match_one, match_two, span):
        self.sources = [in_hbm(x) for x in (adjacency, features, cols, match_one, match_two)]
        self.tables = []
        self.span = span
        self.own, self.other = {}, {}

    def run(self, merges=(), keys=(), leaving=(), apart=(), joint=False, after=(), sums=None):
        adjacency, features, cols, match_one, match_two = self.sources
        rows, width = adjacency.shape[1:]
        plan = Plan()
        plan.rows, plan.depth = rows, rows + HALF + features.shape[0]
        plan.width, plan.sum_depth = width, rows + features.shape[0]
        plan.span, plan.count = self.span, cols.shape[1]
        plan.picks = [(*key, True) for key in leaving] + [(*key, False) for key in keys]
        ins, specs, shapes, scratch = [], [], [], []

        def take(value, spec):
            for place, known in enumerate(ins):
                if known is value:
                    return place
            ins.append(value)
            specs.append(spec)
            return len(ins) - 1

        plan.sources = [take(value, HBM) for value in self.sources] if plan.picks else []
        plan.first = not self.tables
        plan.tables = [take(value, VMEM) for value in self.tables] if plan.picks else []
        if sums is None:
            sums = [[(0, len(merges) * plan.sum_depth)]] if merges else []
        plan.outs = [(None, segments) for segments in sums]

        def needed(i, mains, at):
            first, end = pieces_of(rows // width, len(mains))[at]
            base = i * plan.sum_depth
            return any(plan.place(base + slot * width) for slot in range(first, end))

        plan.merges = [
            [
                (
                    [
                        take(main, VMEM) if needed(i, mains, piece) else None
                        for piece, main in enumerate(mains)
                    ],
                    at,
                    take(side, VMEM),
                    side_at,
                )
                for mains, at, side, side_at in (self.own[key], self.other[key])
            ]
            for i, key in enumerate(merges)
        ]
        for value in after:
            take(value, ANY)

        def give(depth):
            shapes.append(pltpu.VMEM((depth, width), adjacency.dtype))
            return len(ins) + len(shapes) - 1

        plan.outs = [(give(sum(size for _, size in segments)), segments) for segments in sums]
        extra = plan.depth - rows
        if apart:
            ends = len(leaving) * extra
            side = None if joint else give(ends)
            plan.targets = []
            for i, parts in enumerate(apart):
                heights = [(end - first) * width for first, end in pieces_of(rows // width, parts)]
                if i == 0:
                    behind = heights[0] if joint else 0
                    heights[0] += ends if joint else 0
                mains = [give(height) for height in heights]
                side = mains[0] if side is None else side
                plan.targets.append((mains, 0, side, behind + i * extra))
        else:
            mains = [give(plan.depth) for _ in leaving]
            plan.targets = [([main], 0, main, rows) for main in mains]
        if keys:
            pack = give(len(keys) * plan.depth)
            plan.targets += [
                ([pack], i * plan.depth, pack, i * plan.depth + rows) for i in range(len(keys))
            ]
        if plan.first:
            for table in (match_one, match_two):
                plan.tables.append(len(ins) + len(shapes))
                shapes.append(pltpu.VMEM(table.shape, table.dtype))
        plan.sems, total = [], 3
        for mains, _, _, _ in plan.targets:
            plan.sems.append(total)
            total += len(mains) + 1
        if plan.picks:
            scratch = [
                pltpu.SMEM(cols.shape, jnp.int32),
                pltpu.VMEM((HALF, width), jnp.int32),
                pltpu.VMEM((HALF, width), jnp.int32),
                pltpu.SemaphoreType.DMA((total,)),
            ]
        plan.scratch = [len(ins) + len(shapes) + i for i in range(len(scratch))]
        outs = pl.pallas_call(
            lambda *refs: work_kernel(plan, refs),
            out_shape=shapes,
            in_specs=specs,
            out_specs=[VMEM] * len(shapes),
            scratch_shapes=scratch,
            compiler_params=pltpu.CompilerParams(vmem_limit_bytes=LIMIT),
            cost_estimate=LIGHT,
            name="work",
        )(*ins)
        made = {len(ins) + i: value for i, value in enumerate(outs)}
        if plan.first:
            self.tables = [in_vmem(made[at]) for at in plan.tables]
        crossed = {}
        for pick, (mains, main_at, side, side_at) in zip(plan.picks, plan.targets):
            where = self.other if pick[2] else self.own
            for place in (*mains, side):
                if place not in crossed:
                    value = swapped(made[place], "sub") if pick[2] else made[place]
                    crossed[place] = in_vmem(value)
            where[pick[:2]] = ([crossed[main] for main in mains], main_at, crossed[side], side_at)
        return list(outs[: len(sums)] if merges else outs)


def add_kernel(segments, depth, rows, arrived, kept, *rest):
    tiles_out, feats_out, total, sems = rest[-4:]
    width = arrived.shape[-1]
    copies = []
    begin = 0
    for first, size in segments:
        for tile in range(first // depth, -(-(first + size) // depth)):
            for low, high in ((0, rows), (rows, depth)):
                low, high = max(first, tile * depth + low), min(first + size, tile * depth + high)
                if low >= high:
                    continue
                at = begin + low - first
                value = kept[low:high].astype(jnp.float32)
                value += arrived[at : at + high - low].astype(jnp.float32)
                total[at : at + high - low] = value.astype(jnp.bfloat16)
                if high - tile * depth > rows:
                    target = feats_out.at[:, pl.ds(tile * width, width)]
                else:
                    target = tiles_out.at[tile, pl.ds(low - tile * depth, high - low)]
                source = total.at[pl.ds(at, high - low)]
                copies.append(start(source, target, sems.at[len(copies)]))
        begin += size
    for copy in copies:
        copy.wait()


def added(segments, depth, rows, arrived, kept, before):
    size, width = arrived.shape
    quarter = kept.shape[0] // depth
    shapes = (
        jax.ShapeDtypeStruct((quarter, rows, width), jnp.bfloat16),
        jax.ShapeDtypeStruct((depth - rows, quarter * width), jnp.bfloat16),
    )
    return pl.pallas_call(
        functools.partial(add_kernel, segments, depth, rows),
        out_shape=shapes,
        in_specs=[VMEM, VMEM] + [HBM] * len(before),
        out_specs=(HBM, HBM),
        scratch_shapes=[
            pltpu.VMEM((size, width), jnp.bfloat16),
            pltpu.SemaphoreType.DMA((2 * quarter + len(segments),)),
        ],
        input_output_aliases={2: 0, 3: 1} if before else {},
        compiler_params=pltpu.CompilerParams(vmem_limit_bytes=LIMIT),
        cost_estimate=LIGHT,
        name="add",
    )(in_vmem(arrived), in_vmem(kept), *before)


def per_device(features, adjacency, col_tiles, match_one, match_two):
    count, slots, width = adjacency.shape[:3]
    feat_count = features.shape[0]
    quarter = count // 4
    span = lax.axis_size("sub") * count
    blocks = adjacency.reshape(count, slots * width, width)
    work = Work(features, blocks, col_tiles.T, match_one, match_two, span)

    send = [(0, piece) for piece in range(quarter)]
    keep = [(1, piece) for piece in range(quarter)]
    rows = slots * width
    depth = rows + feat_count
    half = slots // 2 * width
    work.run(keys=send[:2], leaving=send[:2], apart=[2, 2], joint=True)
    cut = 3 * depth + 5 * slots // 8 * width
    parts = [
        [(0, half), (rows, feat_count)],
        [(half, rows - half), (depth, depth)],
        [(2 * depth, cut - 2 * depth)],
        [(cut, quarter * depth - cut)],
    ]
    arrived = []

    def merge(keys, which, after):
        base = keys[0][1] * depth
        sums = [[(first - base, size) for first, size in parts[at]] for at in which]
        parcels = work.run(merges=keys, sums=sums, after=after)
        arrived.extend(crossed_over(parcel) for parcel in parcels)
        return parcels

    parcels = merge(send[:1], [0], [])
    parcels = merge(send[:2], [1], parcels)
    work.run(
        keys=send[2:], leaving=send[2:], apart=[1] * (quarter - 2), joint=True,
        after=parcels + arrived[:1],
    )
    parcels = merge(send[2:], [2, 3], [])
    last = work.run(
        keys=keep, leaving=keep, apart=[1] * quarter, after=parcels[:1] + arrived[1:2]
    )
    kept = work.run(merges=keep, after=last[:1])[0]
    out = []
    for segments, part in zip(parts, arrived):
        out = added(segments, depth, rows, part, kept, out)
    return out[0].reshape(quarter, slots, width, width), out[1]


def solution(mesh):
    placed = (
        P(None, ("blk", "sub")),
        P(("blk", "sub"), None, None, None),
        P(("blk", "sub"), None),
        P(),
        P(),
    )
    return jax.shard_map(
        per_device,
        mesh=mesh,
        in_specs=placed,
        out_specs=(P(("blk", "sub"), None, None, None), P(None, ("blk", "sub"))),
        check_vma=False,
    )
```

```python
import functools

import jax
import jax.numpy as jnp
from jax import lax
from jax.experimental import pallas as pl
from jax.experimental.pallas import tpu as pltpu
from jax.sharding import PartitionSpec as P

HALF = 16
LIMIT = 48 * 2**20
LIGHT = pl.CostEstimate(flops=1, bytes_accessed=1, transcendentals=0)
VMEM = pl.BlockSpec(memory_space=pltpu.VMEM)
HBM = pl.BlockSpec(memory_space=pltpu.HBM)
ANY = pl.BlockSpec(memory_space=pl.ANY)


def swapped(value, axis):
    pairs = [(source, source ^ 1) for source in range(lax.axis_size(axis))]
    return lax.ppermute(value, axis, pairs)


def crossed_over(value):
    subs = lax.axis_size("sub")
    count = lax.axis_size("blk") * subs
    pairs = [(at, (at // subs ^ 1) * subs + (at % subs ^ 1)) for at in range(count)]
    return lax.ppermute(value, ("blk", "sub"), pairs)


def in_vmem(value):
    return pltpu.with_memory_space_constraint(value, pltpu.VMEM)


def in_hbm(value):
    return pltpu.with_memory_space_constraint(value, pltpu.HBM)


def split_by(value, size):
    if size & (size - 1) == 0:
        return value >> (size.bit_length() - 1), value & (size - 1)
    return value // size, value % size


def pieces_of(slots, count):
    edges = [slots * at // count for at in range(count + 1)]
    return list(zip(edges, edges[1:]))


def tile_at(phase, piece, partner):
    blk_bit = lax.axis_index("blk") & 1
    sub_bit = lax.axis_index("sub") & 1
    if phase == 0:
        blk_bit = 1 - blk_bit
    if partner == (phase == 1):
        sub_bit = 1 - sub_bit
    return 4 * piece + 2 * blk_bit + sub_bit


def start(source, target, sem):
    copy = pltpu.make_async_copy(source, target, sem)
    copy.start()
    return copy


def compose_maps(pick, span, count, cols, one_table, two_table, one_rows, two_rows, out):
    slots = cols.shape[0]
    lanes = lax.broadcasted_iota(jnp.int32, (1, one_table.shape[-1]), 1)

    def put(row, column_id):
        block, inside = split_by(column_id, span)
        pair_block, high_one = split_by(block, 2)
        sub, place = split_by(inside, count)
        sub_pair, high_two = split_by(sub, 2)
        pair = pair_block * span + inside
        group = pair_block * (span // 2) + sub_pair * count + place
        one_rows[pl.ds(row, 1), :] = jnp.where(high_one == 1, one_table[pl.ds(pair, 1), :], lanes)
        two_rows[pl.ds(row, 1), :] = jnp.where(high_two == 1, two_table[pl.ds(group, 1), :], lanes)

    one_rows[...] = jnp.zeros_like(one_rows)
    two_rows[...] = jnp.zeros_like(two_rows)
    tile = tile_at(*pick)
    for slot in range(slots):
        put(slot, cols[slot, tile])
    put(slots, lax.axis_index("blk") * span + lax.axis_index("sub") * count + tile)
    maps = jnp.take_along_axis(two_rows[...], one_rows[...], axis=1)
    out[...] = maps.astype(jnp.float32).astype(out.dtype)


def merge_tile(slots, width, own, other, own_side, other_side, wanted, put):
    along = lax.broadcasted_iota(jnp.int32, (width, width), 0).astype(jnp.float32)
    own_maps, other_maps = (x[:HALF].astype(jnp.float32) for x in (own_side, other_side))

    def hot(maps, row):
        return (maps[row : row + 1, :] == along).astype(jnp.bfloat16)

    def columns(row):
        return jnp.concatenate([hot(own_maps, row), hot(other_maps, row)], 1)

    def across(value, row):
        return lax.dot_general(
            value, columns(row), (((1,), (1,)), ((), ())), preferred_element_type=jnp.float32
        )

    def block_of(parts, slot):
        for part, (first, end) in zip(parts, pieces_of(slots, len(parts))):
            if first <= slot < end:
                return part[(slot - first) * width : (slot - first + 1) * width, :]

    def moved(rows_hot, tile, pair):
        blocks = [block_of(tile, slot) for slot in (2 * pair, 2 * pair + 1)]
        value = jnp.dot(
            rows_hot, jnp.concatenate(blocks, 1), preferred_element_type=jnp.float32
        ).astype(jnp.bfloat16)
        return [value[:, :width], value[:, width:]]

    own_rows, other_rows = hot(own_maps, slots), hot(other_maps, slots)
    rows_done = {}
    for pair in range(slots // 2):
        if wanted(2 * pair * width):
            halves = moved(own_rows, own, pair), moved(other_rows, other, pair)
            for at, both in enumerate(zip(*halves)):
                rows_done[2 * pair + at] = jnp.concatenate(both, 1)
    for slot, value in rows_done.items():
        put(slot * width, across(value, slot).astype(jnp.bfloat16))
    if wanted(slots * width):
        feats = jnp.concatenate([own_side[HALF:], other_side[HALF:]], 1)
        put(slots * width, across(feats, slots).astype(jnp.bfloat16))


def work_kernel(plan, refs):
    rows = plan.rows
    copies, small = [], []
    if plan.picks:
        adjacency, features, cols, match_one, match_two = [refs[at] for at in plan.sources]
        cols_here, one_rows, two_rows, sems = [refs[at] for at in plan.scratch]
        one_table, two_table = [refs[at] for at in plan.tables]
        width = adjacency.shape[-1]
        small = [start(cols, cols_here, sems.at[2])]
        if plan.first:
            small += [
                start(match_one, one_table, sems.at[0]),
                start(match_two, two_table, sems.at[1]),
            ]
        sides = []
        for i, (pick, (mains, main_at, side, side_at)) in enumerate(zip(plan.picks, plan.targets)):
            tile = tile_at(*pick)
            lanes = pl.ds(pl.multiple_of(tile * width, width), width)
            sides.append(refs[side].at[pl.ds(side_at, HALF)])
            for at, (first, end) in enumerate(pieces_of(rows // width, len(mains))):
                size = (end - first) * width
                copies.append(
                    start(
                        adjacency.at[tile, pl.ds(first * width, size)],
                        refs[mains[at]].at[pl.ds(main_at, size)],
                        sems.at[plan.sems[i] + at],
                    )
                )
            copies.append(
                start(
                    features.at[:, lanes],
                    refs[side].at[pl.ds(side_at + HALF, features.shape[0])],
                    sems.at[plan.sems[i] + len(mains)],
                )
            )
    for i, (own, other) in enumerate(plan.merges):
        tiles = [
            [
                None if main is None else refs[main].at[pl.ds(at, (end - first) * plan.width)]
                for main, (first, end) in zip(mains, pieces_of(rows // plan.width, len(mains)))
            ]
            for mains, at, _, _ in (own, other)
        ]
        ends = [refs[side][at : at + plan.depth - rows, :] for _, _, side, at in (own, other)]

        def wanted(row, base=i * plan.sum_depth):
            return plan.place(base + row) is not None

        def put(row, value, base=i * plan.sum_depth):
            out, at = plan.place(base + row)
            refs[out][pl.ds(at, value.shape[0]), :] = value

        merge_tile(rows // plan.width, plan.width, *tiles, *ends, wanted, put)
    for copy in small:
        copy.wait()
    for i, pick in enumerate(plan.picks):
        compose_maps(
            pick, plan.span, plan.count, cols_here, one_table, two_table, one_rows, two_rows,
            sides[i],
        )
    for copy in copies:
        copy.wait()


class Plan:
    def place(self, row):
        for out, segments in self.outs:
            at = 0
            for first, size in segments:
                if first <= row < first + size:
                    return out, at + row - first
                at += size
        return None


class Work:
    def __init__(self, features, adjacency, cols, match_one, match_two, span):
        self.sources = [in_hbm(x) for x in (adjacency, features, cols, match_one, match_two)]
        self.tables = []
        self.span = span
        self.own, self.other = {}, {}

    def run(self, merges=(), keys=(), leaving=(), apart=(), joint=False, after=(), sums=None):
        adjacency, features, cols, match_one, match_two = self.sources
        rows, width = adjacency.shape[1:]
        plan = Plan()
        plan.rows, plan.depth = rows, rows + HALF + features.shape[0]
        plan.width, plan.sum_depth = width, rows + features.shape[0]
        plan.span, plan.count = self.span, cols.shape[1]
        plan.picks = [(*key, True) for key in leaving] + [(*key, False) for key in keys]
        ins, specs, shapes, scratch = [], [], [], []

        def take(value, spec):
            for place, known in enumerate(ins):
                if known is value:
                    return place
            ins.append(value)
            specs.append(spec)
            return len(ins) - 1

        plan.sources = [take(value, HBM) for value in self.sources] if plan.picks else []
        plan.first = not self.tables
        plan.tables = [take(value, VMEM) for value in self.tables] if plan.picks else []
        if sums is None:
            sums = [[(0, len(merges) * plan.sum_depth)]] if merges else []
        plan.outs = [(None, segments) for segments in sums]

        def needed(i, mains, at):
            first, end = pieces_of(rows // width, len(mains))[at]
            base = i * plan.sum_depth
            return any(plan.place(base + slot * width) for slot in range(first, end))

        plan.merges = [
            [
                (
                    [
                        take(main, VMEM) if needed(i, mains, piece) else None
                        for piece, main in enumerate(mains)
                    ],
                    at,
                    take(side, VMEM),
                    side_at,
                )
                for mains, at, side, side_at in (self.own[key], self.other[key])
            ]
            for i, key in enumerate(merges)
        ]
        for value in after:
            take(value, ANY)

        def give(depth):
            shapes.append(pltpu.VMEM((depth, width), adjacency.dtype))
            return len(ins) + len(shapes) - 1

        plan.outs = [(give(sum(size for _, size in segments)), segments) for segments in sums]
        extra = plan.depth - rows
        if apart:
            ends = len(leaving) * extra
            side = None if joint else give(ends)
            plan.targets = []
            for i, parts in enumerate(apart):
                heights = [(end - first) * width for first, end in pieces_of(rows // width, parts)]
                if i == 0:
                    behind = heights[0] if joint else 0
                    heights[0] += ends if joint else 0
                mains = [give(height) for height in heights]
                side = mains[0] if side is None else side
                plan.targets.append((mains, 0, side, behind + i * extra))
        else:
            mains = [give(plan.depth) for _ in leaving]
            plan.targets = [([main], 0, main, rows) for main in mains]
        if keys:
            pack = give(len(keys) * plan.depth)
            plan.targets += [
                ([pack], i * plan.depth, pack, i * plan.depth + rows) for i in range(len(keys))
            ]
        if plan.first:
            for table in (match_one, match_two):
                plan.tables.append(len(ins) + len(shapes))
                shapes.append(pltpu.VMEM(table.shape, table.dtype))
        plan.sems, total = [], 3
        for mains, _, _, _ in plan.targets:
            plan.sems.append(total)
            total += len(mains) + 1
        if plan.picks:
            scratch = [
                pltpu.SMEM(cols.shape, jnp.int32),
                pltpu.VMEM((HALF, width), jnp.int32),
                pltpu.VMEM((HALF, width), jnp.int32),
                pltpu.SemaphoreType.DMA((total,)),
            ]
        plan.scratch = [len(ins) + len(shapes) + i for i in range(len(scratch))]
        outs = pl.pallas_call(
            lambda *refs: work_kernel(plan, refs),
            out_shape=shapes,
            in_specs=specs,
            out_specs=[VMEM] * len(shapes),
            scratch_shapes=scratch,
            compiler_params=pltpu.CompilerParams(vmem_limit_bytes=LIMIT),
            cost_estimate=LIGHT,
            name="work",
        )(*ins)
        made = {len(ins) + i: value for i, value in enumerate(outs)}
        if plan.first:
            self.tables = [in_vmem(made[at]) for at in plan.tables]
        crossed = {}
        for pick, (mains, main_at, side, side_at) in zip(plan.picks, plan.targets):
            where = self.other if pick[2] else self.own
            for place in (*mains, side):
                if place not in crossed:
                    value = swapped(made[place], "sub") if pick[2] else made[place]
                    crossed[place] = in_vmem(value)
            where[pick[:2]] = ([crossed[main] for main in mains], main_at, crossed[side], side_at)
        return list(outs[: len(sums)] if merges else outs)


def add_kernel(segments, depth, rows, arrived, kept, *rest):
    tiles_out, feats_out, total, sems = rest[-4:]
    width = arrived.shape[-1]
    copies = []
    begin = 0
    for first, size in segments:
        for tile in range(first // depth, -(-(first + size) // depth)):
            for low, high in ((0, rows), (rows, depth)):
                low, high = max(first, tile * depth + low), min(first + size, tile * depth + high)
                if low >= high:
                    continue
                at = begin + low - first
                value = kept[low:high].astype(jnp.float32)
                value += arrived[at : at + high - low].astype(jnp.float32)
                total[at : at + high - low] = value.astype(jnp.bfloat16)
                if high - tile * depth > rows:
                    target = feats_out.at[:, pl.ds(tile * width, width)]
                else:
                    target = tiles_out.at[tile, pl.ds(low - tile * depth, high - low)]
                source = total.at[pl.ds(at, high - low)]
                copies.append(start(source, target, sems.at[len(copies)]))
        begin += size
    for copy in copies:
        copy.wait()


def added(segments, depth, rows, arrived, kept, before):
    size, width = arrived.shape
    quarter = kept.shape[0] // depth
    shapes = (
        jax.ShapeDtypeStruct((quarter, rows, width), jnp.bfloat16),
        jax.ShapeDtypeStruct((depth - rows, quarter * width), jnp.bfloat16),
    )
    return pl.pallas_call(
        functools.partial(add_kernel, segments, depth, rows),
        out_shape=shapes,
        in_specs=[VMEM, VMEM] + [HBM] * len(before),
        out_specs=(HBM, HBM),
        scratch_shapes=[
            pltpu.VMEM((size, width), jnp.bfloat16),
            pltpu.SemaphoreType.DMA((2 * quarter + len(segments),)),
        ],
        input_output_aliases={2: 0, 3: 1} if before else {},
        compiler_params=pltpu.CompilerParams(vmem_limit_bytes=LIMIT),
        cost_estimate=LIGHT,
        name="add",
    )(in_vmem(arrived), in_vmem(kept), *before)


def per_device(features, adjacency, col_tiles, match_one, match_two):
    count, slots, width = adjacency.shape[:3]
    feat_count = features.shape[0]
    quarter = count // 4
    span = lax.axis_size("sub") * count
    blocks = adjacency.reshape(count, slots * width, width)
    work = Work(features, blocks, col_tiles.T, match_one, match_two, span)

    send = [(0, piece) for piece in range(quarter)]
    keep = [(1, piece) for piece in range(quarter)]
    rows = slots * width
    depth = rows + feat_count
    half = slots // 2 * width
    first = work.run(leaving=send[:2])
    work.run(keys=send[:2], after=first[:1])
    cut = 3 * depth + 5 * slots // 8 * width
    parts = [
        [(0, half), (rows, feat_count)],
        [(half, rows - half), (depth, depth)],
        [(2 * depth, cut - 2 * depth)],
        [(cut, quarter * depth - cut)],
    ]
    arrived = []

    def merge(keys, which, after):
        base = keys[0][1] * depth
        sums = [[(first - base, size) for first, size in parts[at]] for at in which]
        parcels = work.run(merges=keys, sums=sums, after=after)
        arrived.extend(crossed_over(parcel) for parcel in parcels)
        return parcels

    parcels = merge(send[:1], [0], [])
    parcels = merge(send[:2], [1], parcels)
    work.run(
        keys=send[2:], leaving=send[2:], apart=[1] * (quarter - 2), joint=True,
        after=parcels + arrived[:1],
    )
    parcels = merge(send[2:], [2, 3], [])
    last = work.run(
        keys=keep, leaving=keep, apart=[1] * quarter, after=parcels[:1] + arrived[1:2]
    )
    kept = work.run(merges=keep, after=last[:1])[0]
    out = []
    for segments, part in zip(parts, arrived):
        out = added(segments, depth, rows, part, kept, out)
    return out[0].reshape(quarter, slots, width, width), out[1]


def solution(mesh):
    placed = (
        P(None, ("blk", "sub")),
        P(("blk", "sub"), None, None, None),
        P(("blk", "sub"), None),
        P(),
        P(),
    )
    return jax.shard_map(
        per_device,
        mesh=mesh,
        in_specs=placed,
        out_specs=(P(("blk", "sub"), None, None, None), P(None, ("blk", "sub"))),
        check_vma=False,
    )
```

```python
import functools

import jax
import jax.numpy as jnp
from jax import lax
from jax.experimental import pallas as pl
from jax.experimental.pallas import tpu as pltpu
from jax.sharding import PartitionSpec as P

HALF = 16
LIMIT = 48 * 2**20
LIGHT = pl.CostEstimate(flops=1, bytes_accessed=1, transcendentals=0)
VMEM = pl.BlockSpec(memory_space=pltpu.VMEM)
HBM = pl.BlockSpec(memory_space=pltpu.HBM)
ANY = pl.BlockSpec(memory_space=pl.ANY)


def swapped(value, axis):
    pairs = [(source, source ^ 1) for source in range(lax.axis_size(axis))]
    return lax.ppermute(value, axis, pairs)


def crossed_over(value):
    subs = lax.axis_size("sub")
    count = lax.axis_size("blk") * subs
    pairs = [(at, (at // subs ^ 1) * subs + (at % subs ^ 1)) for at in range(count)]
    return lax.ppermute(value, ("blk", "sub"), pairs)


def in_vmem(value):
    return pltpu.with_memory_space_constraint(value, pltpu.VMEM)


def in_hbm(value):
    return pltpu.with_memory_space_constraint(value, pltpu.HBM)


def split_by(value, size):
    if size & (size - 1) == 0:
        return value >> (size.bit_length() - 1), value & (size - 1)
    return value // size, value % size


def pieces_of(slots, count):
    edges = [slots * at // count for at in range(count + 1)]
    return list(zip(edges, edges[1:]))


def tile_at(phase, piece, partner):
    blk_bit = lax.axis_index("blk") & 1
    sub_bit = lax.axis_index("sub") & 1
    if phase == 0:
        blk_bit = 1 - blk_bit
    if partner == (phase == 1):
        sub_bit = 1 - sub_bit
    return 4 * piece + 2 * blk_bit + sub_bit


def start(source, target, sem):
    copy = pltpu.make_async_copy(source, target, sem)
    copy.start()
    return copy


def compose_maps(pick, span, count, cols, one_table, two_table, one_rows, two_rows, out):
    slots = cols.shape[0]
    lanes = lax.broadcasted_iota(jnp.int32, (1, one_table.shape[-1]), 1)

    def put(row, column_id):
        block, inside = split_by(column_id, span)
        pair_block, high_one = split_by(block, 2)
        sub, place = split_by(inside, count)
        sub_pair, high_two = split_by(sub, 2)
        pair = pair_block * span + inside
        group = pair_block * (span // 2) + sub_pair * count + place
        one_rows[pl.ds(row, 1), :] = jnp.where(high_one == 1, one_table[pl.ds(pair, 1), :], lanes)
        two_rows[pl.ds(row, 1), :] = jnp.where(high_two == 1, two_table[pl.ds(group, 1), :], lanes)

    one_rows[...] = jnp.zeros_like(one_rows)
    two_rows[...] = jnp.zeros_like(two_rows)
    tile = tile_at(*pick)
    for slot in range(slots):
        put(slot, cols[slot, tile])
    put(slots, lax.axis_index("blk") * span + lax.axis_index("sub") * count + tile)
    maps = jnp.take_along_axis(two_rows[...], one_rows[...], axis=1)
    out[...] = maps.astype(jnp.float32).astype(out.dtype)


def merge_tile(slots, width, own, other, own_side, other_side, wanted, put):
    along = lax.broadcasted_iota(jnp.int32, (width, width), 0).astype(jnp.float32)
    own_maps, other_maps = (x[:HALF].astype(jnp.float32) for x in (own_side, other_side))

    def hot(maps, row):
        return (maps[row : row + 1, :] == along).astype(jnp.bfloat16)

    def columns(row):
        return jnp.concatenate([hot(own_maps, row), hot(other_maps, row)], 1)

    def across(value, row):
        return lax.dot_general(
            value, columns(row), (((1,), (1,)), ((), ())), preferred_element_type=jnp.float32
        )

    def block_of(parts, slot):
        for part, (first, end) in zip(parts, pieces_of(slots, len(parts))):
            if first <= slot < end:
                return part[(slot - first) * width : (slot - first + 1) * width, :]

    def moved(rows_hot, tile, pair):
        blocks = [block_of(tile, slot) for slot in (2 * pair, 2 * pair + 1)]
        value = jnp.dot(
            rows_hot, jnp.concatenate(blocks, 1), preferred_element_type=jnp.float32
        ).astype(jnp.bfloat16)
        return [value[:, :width], value[:, width:]]

    own_rows, other_rows = hot(own_maps, slots), hot(other_maps, slots)
    rows_done = {}
    for pair in range(slots // 2):
        if wanted(2 * pair * width):
            halves = moved(own_rows, own, pair), moved(other_rows, other, pair)
            for at, both in enumerate(zip(*halves)):
                rows_done[2 * pair + at] = jnp.concatenate(both, 1)
    for slot, value in rows_done.items():
        put(slot * width, across(value, slot).astype(jnp.bfloat16))
    if wanted(slots * width):
        feats = jnp.concatenate([own_side[HALF:], other_side[HALF:]], 1)
        put(slots * width, across(feats, slots).astype(jnp.bfloat16))


def work_kernel(plan, refs):
    rows = plan.rows
    copies, small = [], []
    if plan.picks:
        adjacency, features, cols, match_one, match_two = [refs[at] for at in plan.sources]
        cols_here, one_rows, two_rows, sems = [refs[at] for at in plan.scratch]
        one_table, two_table = [refs[at] for at in plan.tables]
        width = adjacency.shape[-1]
        small = [start(cols, cols_here, sems.at[2])]
        if plan.first:
            small += [
                start(match_one, one_table, sems.at[0]),
                start(match_two, two_table, sems.at[1]),
            ]
        sides = []
        for i, (pick, (mains, main_at, side, side_at)) in enumerate(zip(plan.picks, plan.targets)):
            tile = tile_at(*pick)
            lanes = pl.ds(pl.multiple_of(tile * width, width), width)
            sides.append(refs[side].at[pl.ds(side_at, HALF)])
            for at, (first, end) in enumerate(pieces_of(rows // width, len(mains))):
                size = (end - first) * width
                copies.append(
                    start(
                        adjacency.at[tile, pl.ds(first * width, size)],
                        refs[mains[at]].at[pl.ds(main_at, size)],
                        sems.at[plan.sems[i] + at],
                    )
                )
            copies.append(
                start(
                    features.at[:, lanes],
                    refs[side].at[pl.ds(side_at + HALF, features.shape[0])],
                    sems.at[plan.sems[i] + len(mains)],
                )
            )
    for i, (own, other) in enumerate(plan.merges):
        tiles = [
            [
                None if main is None else refs[main].at[pl.ds(at, (end - first) * plan.width)]
                for main, (first, end) in zip(mains, pieces_of(rows // plan.width, len(mains)))
            ]
            for mains, at, _, _ in (own, other)
        ]
        ends = [refs[side][at : at + plan.depth - rows, :] for _, _, side, at in (own, other)]

        def wanted(row, base=i * plan.sum_depth):
            return plan.place(base + row) is not None

        def put(row, value, base=i * plan.sum_depth):
            out, at = plan.place(base + row)
            refs[out][pl.ds(at, value.shape[0]), :] = value

        merge_tile(rows // plan.width, plan.width, *tiles, *ends, wanted, put)
    for copy in small:
        copy.wait()
    for i, pick in enumerate(plan.picks):
        compose_maps(
            pick, plan.span, plan.count, cols_here, one_table, two_table, one_rows, two_rows,
            sides[i],
        )
    for copy in copies:
        copy.wait()


class Plan:
    def place(self, row):
        for out, segments in self.outs:
            at = 0
            for first, size in segments:
                if first <= row < first + size:
                    return out, at + row - first
                at += size
        return None


class Work:
    def __init__(self, features, adjacency, cols, match_one, match_two, span):
        self.sources = [in_hbm(x) for x in (adjacency, features, cols, match_one, match_two)]
        self.tables = []
        self.span = span
        self.own, self.other = {}, {}

    def run(self, merges=(), keys=(), leaving=(), apart=(), joint=False, after=(), sums=None):
        adjacency, features, cols, match_one, match_two = self.sources
        rows, width = adjacency.shape[1:]
        plan = Plan()
        plan.rows, plan.depth = rows, rows + HALF + features.shape[0]
        plan.width, plan.sum_depth = width, rows + features.shape[0]
        plan.span, plan.count = self.span, cols.shape[1]
        plan.picks = [(*key, True) for key in leaving] + [(*key, False) for key in keys]
        ins, specs, shapes, scratch = [], [], [], []

        def take(value, spec):
            for place, known in enumerate(ins):
                if known is value:
                    return place
            ins.append(value)
            specs.append(spec)
            return len(ins) - 1

        plan.sources = [take(value, HBM) for value in self.sources] if plan.picks else []
        plan.first = not self.tables
        plan.tables = [take(value, VMEM) for value in self.tables] if plan.picks else []
        if sums is None:
            sums = [[(0, len(merges) * plan.sum_depth)]] if merges else []
        plan.outs = [(None, segments) for segments in sums]

        def needed(i, mains, at):
            first, end = pieces_of(rows // width, len(mains))[at]
            base = i * plan.sum_depth
            return any(plan.place(base + slot * width) for slot in range(first, end))

        plan.merges = [
            [
                (
                    [
                        take(main, VMEM) if needed(i, mains, piece) else None
                        for piece, main in enumerate(mains)
                    ],
                    at,
                    take(side, VMEM),
                    side_at,
                )
                for mains, at, side, side_at in (self.own[key], self.other[key])
            ]
            for i, key in enumerate(merges)
        ]
        for value in after:
            take(value, ANY)

        def give(depth):
            shapes.append(pltpu.VMEM((depth, width), adjacency.dtype))
            return len(ins) + len(shapes) - 1

        plan.outs = [(give(sum(size for _, size in segments)), segments) for segments in sums]
        extra = plan.depth - rows
        if apart:
            ends = len(leaving) * extra
            side = None if joint else give(ends)
            plan.targets = []
            for i, parts in enumerate(apart):
                heights = [(end - first) * width for first, end in pieces_of(rows // width, parts)]
                if i == 0:
                    behind = heights[0] if joint else 0
                    heights[0] += ends if joint else 0
                mains = [give(height) for height in heights]
                side = mains[0] if side is None else side
                plan.targets.append((mains, 0, side, behind + i * extra))
        else:
            mains = [give(plan.depth) for _ in leaving]
            plan.targets = [([main], 0, main, rows) for main in mains]
        if keys:
            pack = give(len(keys) * plan.depth)
            plan.targets += [
                ([pack], i * plan.depth, pack, i * plan.depth + rows) for i in range(len(keys))
            ]
        if plan.first:
            for table in (match_one, match_two):
                plan.tables.append(len(ins) + len(shapes))
                shapes.append(pltpu.VMEM(table.shape, table.dtype))
        plan.sems, total = [], 3
        for mains, _, _, _ in plan.targets:
            plan.sems.append(total)
            total += len(mains) + 1
        if plan.picks:
            scratch = [
                pltpu.SMEM(cols.shape, jnp.int32),
                pltpu.VMEM((HALF, width), jnp.int32),
                pltpu.VMEM((HALF, width), jnp.int32),
                pltpu.SemaphoreType.DMA((total,)),
            ]
        plan.scratch = [len(ins) + len(shapes) + i for i in range(len(scratch))]
        outs = pl.pallas_call(
            lambda *refs: work_kernel(plan, refs),
            out_shape=shapes,
            in_specs=specs,
            out_specs=[VMEM] * len(shapes),
            scratch_shapes=scratch,
            compiler_params=pltpu.CompilerParams(vmem_limit_bytes=LIMIT),
            cost_estimate=LIGHT,
            name="work",
        )(*ins)
        made = {len(ins) + i: value for i, value in enumerate(outs)}
        if plan.first:
            self.tables = [in_vmem(made[at]) for at in plan.tables]
        crossed = {}
        for pick, (mains, main_at, side, side_at) in zip(plan.picks, plan.targets):
            where = self.other if pick[2] else self.own
            for place in (*mains, side):
                if place not in crossed:
                    value = swapped(made[place], "sub") if pick[2] else made[place]
                    crossed[place] = in_vmem(value)
            where[pick[:2]] = ([crossed[main] for main in mains], main_at, crossed[side], side_at)
        return list(outs[: len(sums)] if merges else outs)


def add_kernel(parts, depth, rows, *refs):
    tiles_out, feats_out, total, sems = refs[-4:]
    kept = refs[len(parts)]
    width = kept.shape[-1]
    copies = []
    begin = 0
    listed = []
    for segments, arrived in zip(parts, refs):
        top = begin
        for first, size in segments:
            listed.append((arrived, top, first, size, begin))
            begin += size
    for arrived, top, first, size, begin in listed:
        for tile in range(first // depth, -(-(first + size) // depth)):
            for low, high in ((0, rows), (rows, depth)):
                low, high = max(first, tile * depth + low), min(first + size, tile * depth + high)
                if low >= high:
                    continue
                at = begin + low - first
                value = kept[low:high].astype(jnp.float32)
                value += arrived[at - top : at - top + high - low].astype(jnp.float32)
                total[at : at + high - low] = value.astype(jnp.bfloat16)
                if high - tile * depth > rows:
                    target = feats_out.at[:, pl.ds(tile * width, width)]
                else:
                    target = tiles_out.at[tile, pl.ds(low - tile * depth, high - low)]
                source = total.at[pl.ds(at, high - low)]
                copies.append(start(source, target, sems.at[len(copies)]))
    for copy in copies:
        copy.wait()


def added(parts, depth, rows, arrived, kept, before):
    size, width = sum(part.shape[0] for part in arrived), kept.shape[1]
    quarter = kept.shape[0] // depth
    shapes = (
        jax.ShapeDtypeStruct((quarter, rows, width), jnp.bfloat16),
        jax.ShapeDtypeStruct((depth - rows, quarter * width), jnp.bfloat16),
    )
    return pl.pallas_call(
        functools.partial(add_kernel, parts, depth, rows),
        out_shape=shapes,
        in_specs=[VMEM] * (len(arrived) + 1) + [HBM] * len(before),
        out_specs=(HBM, HBM),
        scratch_shapes=[
            pltpu.VMEM((size, width), jnp.bfloat16),
            pltpu.SemaphoreType.DMA((2 * quarter + sum(map(len, parts)),)),
        ],
        input_output_aliases={len(arrived) + at: at - 1 for at in (1, 2)} if before else {},
        compiler_params=pltpu.CompilerParams(vmem_limit_bytes=LIMIT),
        cost_estimate=LIGHT,
        name="add",
    )(*map(in_vmem, arrived), in_vmem(kept), *before)


def per_device(features, adjacency, col_tiles, match_one, match_two):
    count, slots, width = adjacency.shape[:3]
    feat_count = features.shape[0]
    quarter = count // 4
    span = lax.axis_size("sub") * count
    blocks = adjacency.reshape(count, slots * width, width)
    work = Work(features, blocks, col_tiles.T, match_one, match_two, span)

    send = [(0, piece) for piece in range(quarter)]
    keep = [(1, piece) for piece in range(quarter)]
    rows = slots * width
    depth = rows + feat_count
    half = slots // 2 * width
    first = work.run(leaving=send[:2])
    work.run(keys=send[:2], after=first[:1])
    cut = 3 * depth + 5 * slots // 8 * width
    parts = [
        [(0, half), (rows, feat_count)],
        [(half, rows - half), (depth, depth)],
        [(2 * depth, cut - 2 * depth)],
        [(cut, quarter * depth - cut)],
    ]
    arrived = []

    def merge(keys, which, after):
        base = keys[0][1] * depth
        sums = [[(first - base, size) for first, size in parts[at]] for at in which]
        parcels = work.run(merges=keys, sums=sums, after=after)
        arrived.extend(crossed_over(parcel) for parcel in parcels)
        return parcels

    parcels = merge(send[:1], [0], [])
    parcels = merge(send[:2], [1], parcels)
    work.run(
        keys=send[2:], leaving=send[2:], apart=[1] * (quarter - 2), joint=True,
        after=parcels + arrived[:1],
    )
    parcels = merge(send[2:], [2, 3], [])
    last = work.run(
        keys=keep, leaving=keep, apart=[1] * quarter, after=parcels[:1] + arrived[1:2]
    )
    kept = work.run(merges=keep, after=last[:1])[0]
    out = []
    for low, high in ((0, 2), (2, 3), (3, 4)):
        out = added(parts[low:high], depth, rows, arrived[low:high], kept, out)
    return out[0].reshape(quarter, slots, width, width), out[1]


def solution(mesh):
    placed = (
        P(None, ("blk", "sub")),
        P(("blk", "sub"), None, None, None),
        P(("blk", "sub"), None),
        P(),
        P(),
    )
    return jax.shard_map(
        per_device,
        mesh=mesh,
        in_specs=placed,
        out_specs=(P(("blk", "sub"), None, None, None), P(None, ("blk", "sub"))),
        check_vma=False,
    )
```

```python
import functools

import jax
import jax.numpy as jnp
from jax import lax
from jax.experimental import pallas as pl
from jax.experimental.pallas import tpu as pltpu
from jax.sharding import PartitionSpec as P

HALF = 16
LIMIT = 48 * 2**20
LIGHT = pl.CostEstimate(flops=1, bytes_accessed=1, transcendentals=0)
VMEM = pl.BlockSpec(memory_space=pltpu.VMEM)
HBM = pl.BlockSpec(memory_space=pltpu.HBM)
ANY = pl.BlockSpec(memory_space=pl.ANY)


def swapped(value, axis):
    pairs = [(source, source ^ 1) for source in range(lax.axis_size(axis))]
    return lax.ppermute(value, axis, pairs)


def crossed_over(value):
    subs = lax.axis_size("sub")
    count = lax.axis_size("blk") * subs
    pairs = [(at, (at // subs ^ 1) * subs + (at % subs ^ 1)) for at in range(count)]
    return lax.ppermute(value, ("blk", "sub"), pairs)


def in_vmem(value):
    return pltpu.with_memory_space_constraint(value, pltpu.VMEM)


def in_hbm(value):
    return pltpu.with_memory_space_constraint(value, pltpu.HBM)


def split_by(value, size):
    if size & (size - 1) == 0:
        return value >> (size.bit_length() - 1), value & (size - 1)
    return value // size, value % size


def pieces_of(slots, count):
    edges = [slots * at // count for at in range(count + 1)]
    return list(zip(edges, edges[1:]))


def tile_at(phase, piece, partner):
    blk_bit = lax.axis_index("blk") & 1
    sub_bit = lax.axis_index("sub") & 1
    if phase == 0:
        blk_bit = 1 - blk_bit
    if partner == (phase == 1):
        sub_bit = 1 - sub_bit
    return 4 * piece + 2 * blk_bit + sub_bit


def start(source, target, sem):
    copy = pltpu.make_async_copy(source, target, sem)
    copy.start()
    return copy


def compose_maps(pick, span, count, cols, one_table, two_table, one_rows, two_rows, out):
    slots = cols.shape[0]
    lanes = lax.broadcasted_iota(jnp.int32, (1, one_table.shape[-1]), 1)

    def put(row, column_id):
        block, inside = split_by(column_id, span)
        pair_block, high_one = split_by(block, 2)
        sub, place = split_by(inside, count)
        sub_pair, high_two = split_by(sub, 2)
        pair = pair_block * span + inside
        group = pair_block * (span // 2) + sub_pair * count + place
        one_rows[pl.ds(row, 1), :] = jnp.where(high_one == 1, one_table[pl.ds(pair, 1), :], lanes)
        two_rows[pl.ds(row, 1), :] = jnp.where(high_two == 1, two_table[pl.ds(group, 1), :], lanes)

    one_rows[...] = jnp.zeros_like(one_rows)
    two_rows[...] = jnp.zeros_like(two_rows)
    tile = tile_at(*pick)
    for slot in range(slots):
        put(slot, cols[slot, tile])
    put(slots, lax.axis_index("blk") * span + lax.axis_index("sub") * count + tile)
    maps = jnp.take_along_axis(two_rows[...], one_rows[...], axis=1)
    out[...] = maps.astype(jnp.float32).astype(out.dtype)


def merge_tile(slots, width, own, other, own_side, other_side, wanted, put):
    along = lax.broadcasted_iota(jnp.int32, (width, width), 0).astype(jnp.float32)
    own_maps, other_maps = (x[:HALF].astype(jnp.float32) for x in (own_side, other_side))

    def hot(maps, row):
        return (maps[row : row + 1, :] == along).astype(jnp.bfloat16)

    def columns(row):
        return jnp.concatenate([hot(own_maps, row), hot(other_maps, row)], 1)

    def across(value, row):
        return lax.dot_general(
            value, columns(row), (((1,), (1,)), ((), ())), preferred_element_type=jnp.float32
        )

    def block_of(parts, slot):
        for part, (first, end) in zip(parts, pieces_of(slots, len(parts))):
            if first <= slot < end:
                return part[(slot - first) * width : (slot - first + 1) * width, :]

    def moved(rows_hot, tile, pair):
        blocks = [block_of(tile, slot) for slot in (2 * pair, 2 * pair + 1)]
        value = jnp.dot(
            rows_hot, jnp.concatenate(blocks, 1), preferred_element_type=jnp.float32
        ).astype(jnp.bfloat16)
        return [value[:, :width], value[:, width:]]

    own_rows, other_rows = hot(own_maps, slots), hot(other_maps, slots)
    rows_done = {}
    for pair in range(slots // 2):
        if wanted(2 * pair * width):
            halves = moved(own_rows, own, pair), moved(other_rows, other, pair)
            for at, both in enumerate(zip(*halves)):
                rows_done[2 * pair + at] = jnp.concatenate(both, 1)
    for slot, value in rows_done.items():
        put(slot * width, across(value, slot).astype(jnp.bfloat16))
    if wanted(slots * width):
        feats = jnp.concatenate([own_side[HALF:], other_side[HALF:]], 1)
        put(slots * width, across(feats, slots).astype(jnp.bfloat16))


def work_kernel(plan, refs):
    rows = plan.rows
    copies, small = [], []
    if plan.picks:
        adjacency, features, cols, match_one, match_two = [refs[at] for at in plan.sources]
        cols_here, one_rows, two_rows, sems = [refs[at] for at in plan.scratch]
        one_table, two_table = [refs[at] for at in plan.tables]
        width = adjacency.shape[-1]
        small = [start(cols, cols_here, sems.at[2])]
        if plan.first:
            small += [
                start(match_one, one_table, sems.at[0]),
                start(match_two, two_table, sems.at[1]),
            ]
        sides = []
        for i, (pick, (mains, main_at, side, side_at)) in enumerate(zip(plan.picks, plan.targets)):
            tile = tile_at(*pick)
            lanes = pl.ds(pl.multiple_of(tile * width, width), width)
            sides.append(refs[side].at[pl.ds(side_at, HALF)])
            for at, (first, end) in enumerate(pieces_of(rows // width, len(mains))):
                size = (end - first) * width
                copies.append(
                    start(
                        adjacency.at[tile, pl.ds(first * width, size)],
                        refs[mains[at]].at[pl.ds(main_at, size)],
                        sems.at[plan.sems[i] + at],
                    )
                )
            copies.append(
                start(
                    features.at[:, lanes],
                    refs[side].at[pl.ds(side_at + HALF, features.shape[0])],
                    sems.at[plan.sems[i] + len(mains)],
                )
            )
    for i, (own, other) in enumerate(plan.merges):
        tiles = [
            [
                None if main is None else refs[main].at[pl.ds(at, (end - first) * plan.width)]
                for main, (first, end) in zip(mains, pieces_of(rows // plan.width, len(mains)))
            ]
            for mains, at, _, _ in (own, other)
        ]
        ends = [refs[side][at : at + plan.depth - rows, :] for _, _, side, at in (own, other)]

        def wanted(row, base=i * plan.sum_depth):
            return plan.place(base + row) is not None

        def put(row, value, base=i * plan.sum_depth):
            out, at = plan.place(base + row)
            refs[out][pl.ds(at, value.shape[0]), :] = value

        merge_tile(rows // plan.width, plan.width, *tiles, *ends, wanted, put)
    for copy in small:
        copy.wait()
    for i, pick in enumerate(plan.picks):
        compose_maps(
            pick, plan.span, plan.count, cols_here, one_table, two_table, one_rows, two_rows,
            sides[i],
        )
    for copy in copies:
        copy.wait()


class Plan:
    def place(self, row):
        for out, segments in self.outs:
            at = 0
            for first, size in segments:
                if first <= row < first + size:
                    return out, at + row - first
                at += size
        return None


class Work:
    def __init__(self, features, adjacency, cols, match_one, match_two, span):
        self.sources = [in_hbm(x) for x in (adjacency, features, cols, match_one, match_two)]
        self.tables = []
        self.span = span
        self.own, self.other = {}, {}

    def run(self, merges=(), keys=(), leaving=(), apart=(), joint=False, after=(), sums=None):
        adjacency, features, cols, match_one, match_two = self.sources
        rows, width = adjacency.shape[1:]
        plan = Plan()
        plan.rows, plan.depth = rows, rows + HALF + features.shape[0]
        plan.width, plan.sum_depth = width, rows + features.shape[0]
        plan.span, plan.count = self.span, cols.shape[1]
        plan.picks = [(*key, True) for key in leaving] + [(*key, False) for key in keys]
        ins, specs, shapes, scratch = [], [], [], []

        def take(value, spec):
            for place, known in enumerate(ins):
                if known is value:
                    return place
            ins.append(value)
            specs.append(spec)
            return len(ins) - 1

        plan.sources = [take(value, HBM) for value in self.sources] if plan.picks else []
        plan.first = not self.tables
        plan.tables = [take(value, VMEM) for value in self.tables] if plan.picks else []
        if sums is None:
            sums = [[(0, len(merges) * plan.sum_depth)]] if merges else []
        plan.outs = [(None, segments) for segments in sums]

        def needed(i, mains, at):
            first, end = pieces_of(rows // width, len(mains))[at]
            base = i * plan.sum_depth
            return any(plan.place(base + slot * width) for slot in range(first, end))

        plan.merges = [
            [
                (
                    [
                        take(main, VMEM) if needed(i, mains, piece) else None
                        for piece, main in enumerate(mains)
                    ],
                    at,
                    take(side, VMEM),
                    side_at,
                )
                for mains, at, side, side_at in (self.own[key], self.other[key])
            ]
            for i, key in enumerate(merges)
        ]
        for value in after:
            take(value, ANY)

        def give(depth):
            shapes.append(pltpu.VMEM((depth, width), adjacency.dtype))
            return len(ins) + len(shapes) - 1

        plan.outs = [(give(sum(size for _, size in segments)), segments) for segments in sums]
        extra = plan.depth - rows
        if apart:
            ends = len(leaving) * extra
            side = None if joint else give(ends)
            plan.targets = []
            for i, parts in enumerate(apart):
                heights = [(end - first) * width for first, end in pieces_of(rows // width, parts)]
                if i == 0:
                    behind = heights[0] if joint else 0
                    heights[0] += ends if joint else 0
                mains = [give(height) for height in heights]
                side = mains[0] if side is None else side
                plan.targets.append((mains, 0, side, behind + i * extra))
        else:
            mains = [give(plan.depth) for _ in leaving]
            plan.targets = [([main], 0, main, rows) for main in mains]
        if keys:
            pack = give(len(keys) * plan.depth)
            plan.targets += [
                ([pack], i * plan.depth, pack, i * plan.depth + rows) for i in range(len(keys))
            ]
        if plan.first:
            for table in (match_one, match_two):
                plan.tables.append(len(ins) + len(shapes))
                shapes.append(pltpu.VMEM(table.shape, table.dtype))
        plan.sems, total = [], 3
        for mains, _, _, _ in plan.targets:
            plan.sems.append(total)
            total += len(mains) + 1
        if plan.picks:
            scratch = [
                pltpu.SMEM(cols.shape, jnp.int32),
                pltpu.VMEM((HALF, width), jnp.int32),
                pltpu.VMEM((HALF, width), jnp.int32),
                pltpu.SemaphoreType.DMA((total,)),
            ]
        plan.scratch = [len(ins) + len(shapes) + i for i in range(len(scratch))]
        outs = pl.pallas_call(
            lambda *refs: work_kernel(plan, refs),
            out_shape=shapes,
            in_specs=specs,
            out_specs=[VMEM] * len(shapes),
            scratch_shapes=scratch,
            compiler_params=pltpu.CompilerParams(vmem_limit_bytes=LIMIT),
            cost_estimate=LIGHT,
            name="work",
        )(*ins)
        made = {len(ins) + i: value for i, value in enumerate(outs)}
        if plan.first:
            self.tables = [in_vmem(made[at]) for at in plan.tables]
        crossed = {}
        for pick, (mains, main_at, side, side_at) in zip(plan.picks, plan.targets):
            where = self.other if pick[2] else self.own
            for place in (*mains, side):
                if place not in crossed:
                    value = swapped(made[place], "sub") if pick[2] else made[place]
                    crossed[place] = in_vmem(value)
            where[pick[:2]] = ([crossed[main] for main in mains], main_at, crossed[side], side_at)
        return list(outs[: len(sums)] if merges else outs)


def add_kernel(segments, depth, rows, arrived, kept, *rest):
    tiles_out, feats_out, total, sems = rest[-4:]
    width = arrived.shape[-1]
    copies = []
    begin = 0
    for first, size in segments:
        for tile in range(first // depth, -(-(first + size) // depth)):
            for low, high in ((0, rows), (rows, depth)):
                low, high = max(first, tile * depth + low), min(first + size, tile * depth + high)
                if low >= high:
                    continue
                at = begin + low - first
                value = kept[low:high].astype(jnp.float32)
                value += arrived[at : at + high - low].astype(jnp.float32)
                total[at : at + high - low] = value.astype(jnp.bfloat16)
                if high - tile * depth > rows:
                    target = feats_out.at[:, pl.ds(tile * width, width)]
                else:
                    target = tiles_out.at[tile, pl.ds(low - tile * depth, high - low)]
                source = total.at[pl.ds(at, high - low)]
                copies.append(start(source, target, sems.at[len(copies)]))
        begin += size
    for copy in copies:
        copy.wait()


def added(segments, depth, rows, arrived, kept, before):
    size, width = arrived.shape
    quarter = kept.shape[0] // depth
    shapes = (
        jax.ShapeDtypeStruct((quarter, rows, width), jnp.bfloat16),
        jax.ShapeDtypeStruct((depth - rows, quarter * width), jnp.bfloat16),
    )
    return pl.pallas_call(
        functools.partial(add_kernel, segments, depth, rows),
        out_shape=shapes,
        in_specs=[VMEM, VMEM] + [HBM] * len(before),
        out_specs=(HBM, HBM),
        scratch_shapes=[
            pltpu.VMEM((size, width), jnp.bfloat16),
            pltpu.SemaphoreType.DMA((2 * quarter + len(segments),)),
        ],
        input_output_aliases={2: 0, 3: 1} if before else {},
        compiler_params=pltpu.CompilerParams(vmem_limit_bytes=LIMIT),
        cost_estimate=LIGHT,
        name="add",
    )(in_vmem(arrived), in_vmem(kept), *before)


def per_device(features, adjacency, col_tiles, match_one, match_two):
    count, slots, width = adjacency.shape[:3]
    feat_count = features.shape[0]
    quarter = count // 4
    span = lax.axis_size("sub") * count
    blocks = adjacency.reshape(count, slots * width, width)
    work = Work(features, blocks, col_tiles.T, match_one, match_two, span)

    send = [(0, piece) for piece in range(quarter)]
    keep = [(1, piece) for piece in range(quarter)]
    rows = slots * width
    depth = rows + feat_count
    half = slots // 2 * width
    first = work.run(leaving=send[:2])
    work.run(keys=send[:2], after=first[:1])
    cut = 3 * depth + 5 * slots // 8 * width
    parts = [
        [(0, half), (rows, feat_count)],
        [(half, rows - half), (depth, depth)],
        [(2 * depth, cut - 2 * depth)],
        [(cut, quarter * depth - cut)],
    ]
    arrived = []

    def merge(keys, which, after):
        base = keys[0][1] * depth
        sums = [[(first - base, size) for first, size in parts[at]] for at in which]
        parcels = work.run(merges=keys, sums=sums, after=after)
        arrived.extend(crossed_over(parcel) for parcel in parcels)
        return parcels

    parcels = merge(send[:1], [0], [])
    parcels = merge(send[:2], [1], parcels)
    work.run(
        keys=send[2:], leaving=send[2:], apart=[1] * (quarter - 2), joint=True,
        after=parcels + arrived[:1],
    )
    parcels = merge(send[2:], [2, 3], [])
    last = work.run(
        keys=keep, leaving=keep, apart=[1] * quarter, joint=True, after=parcels[:1] + arrived[1:2]
    )
    kept = work.run(merges=keep, after=last[:1])[0]
    out = []
    for segments, part in zip(parts, arrived):
        out = added(segments, depth, rows, part, kept, out)
    return out[0].reshape(quarter, slots, width, width), out[1]


def solution(mesh):
    placed = (
        P(None, ("blk", "sub")),
        P(("blk", "sub"), None, None, None),
        P(("blk", "sub"), None),
        P(),
        P(),
    )
    return jax.shard_map(
        per_device,
        mesh=mesh,
        in_specs=placed,
        out_specs=(P(("blk", "sub"), None, None, None), P(None, ("blk", "sub"))),
        check_vma=False,
    )
```

```python
import functools

import jax
import jax.numpy as jnp
from jax import lax
from jax.experimental import pallas as pl
from jax.experimental.pallas import tpu as pltpu
from jax.sharding import PartitionSpec as P

HALF = 16
LIMIT = 48 * 2**20
LIGHT = pl.CostEstimate(flops=1, bytes_accessed=1, transcendentals=0)
VMEM = pl.BlockSpec(memory_space=pltpu.VMEM)
HBM = pl.BlockSpec(memory_space=pltpu.HBM)
ANY = pl.BlockSpec(memory_space=pl.ANY)


def swapped(value, axis):
    pairs = [(source, source ^ 1) for source in range(lax.axis_size(axis))]
    return lax.ppermute(value, axis, pairs)


def crossed_over(value):
    subs = lax.axis_size("sub")
    count = lax.axis_size("blk") * subs
    pairs = [(at, (at // subs ^ 1) * subs + (at % subs ^ 1)) for at in range(count)]
    return lax.ppermute(value, ("blk", "sub"), pairs)


def in_vmem(value):
    return pltpu.with_memory_space_constraint(value, pltpu.VMEM)


def in_hbm(value):
    return pltpu.with_memory_space_constraint(value, pltpu.HBM)


def split_by(value, size):
    if size & (size - 1) == 0:
        return value >> (size.bit_length() - 1), value & (size - 1)
    return value // size, value % size


def pieces_of(slots, count):
    edges = [slots * at // count for at in range(count + 1)]
    return list(zip(edges, edges[1:]))


def tile_at(phase, piece, partner):
    blk_bit = lax.axis_index("blk") & 1
    sub_bit = lax.axis_index("sub") & 1
    if phase == 0:
        blk_bit = 1 - blk_bit
    if partner == (phase == 1):
        sub_bit = 1 - sub_bit
    return 4 * piece + 2 * blk_bit + sub_bit


def start(source, target, sem):
    copy = pltpu.make_async_copy(source, target, sem)
    copy.start()
    return copy


def compose_maps(pick, span, count, cols, one_table, two_table, one_rows, two_rows, out):
    slots = cols.shape[0]
    lanes = lax.broadcasted_iota(jnp.int32, (1, one_table.shape[-1]), 1)

    def put(row, column_id):
        block, inside = split_by(column_id, span)
        pair_block, high_one = split_by(block, 2)
        sub, place = split_by(inside, count)
        sub_pair, high_two = split_by(sub, 2)
        pair = pair_block * span + inside
        group = pair_block * (span // 2) + sub_pair * count + place
        one_rows[pl.ds(row, 1), :] = jnp.where(high_one == 1, one_table[pl.ds(pair, 1), :], lanes)
        two_rows[pl.ds(row, 1), :] = jnp.where(high_two == 1, two_table[pl.ds(group, 1), :], lanes)

    one_rows[...] = jnp.zeros_like(one_rows)
    two_rows[...] = jnp.zeros_like(two_rows)
    tile = tile_at(*pick)
    for slot in range(slots):
        put(slot, cols[slot, tile])
    put(slots, lax.axis_index("blk") * span + lax.axis_index("sub") * count + tile)
    maps = jnp.take_along_axis(two_rows[...], one_rows[...], axis=1)
    out[...] = maps.astype(jnp.float32).astype(out.dtype)


def merge_tile(slots, width, own, other, own_side, other_side, wanted, put):
    along = lax.broadcasted_iota(jnp.int32, (width, width), 0).astype(jnp.float32)
    own_maps, other_maps = (x[:HALF].astype(jnp.float32) for x in (own_side, other_side))

    def hot(maps, row):
        return (maps[row : row + 1, :] == along).astype(jnp.bfloat16)

    def columns(row):
        return jnp.concatenate([hot(own_maps, row), hot(other_maps, row)], 1)

    def across(value, row):
        return lax.dot_general(
            value, columns(row), (((1,), (1,)), ((), ())), preferred_element_type=jnp.float32
        )

    def block_of(parts, slot):
        for part, (first, end) in zip(parts, pieces_of(slots, len(parts))):
            if first <= slot < end:
                return part[(slot - first) * width : (slot - first + 1) * width, :]

    def moved(rows_hot, tile, pair):
        blocks = [block_of(tile, slot) for slot in (2 * pair, 2 * pair + 1)]
        value = jnp.dot(
            rows_hot, jnp.concatenate(blocks, 1), preferred_element_type=jnp.float32
        ).astype(jnp.bfloat16)
        return [value[:, :width], value[:, width:]]

    own_rows, other_rows = hot(own_maps, slots), hot(other_maps, slots)
    rows_done = {}
    for pair in range(slots // 2):
        if wanted(2 * pair * width):
            halves = moved(own_rows, own, pair), moved(other_rows, other, pair)
            for at, both in enumerate(zip(*halves)):
                rows_done[2 * pair + at] = jnp.concatenate(both, 1)
    for slot, value in rows_done.items():
        put(slot * width, across(value, slot).astype(jnp.bfloat16))
    if wanted(slots * width):
        feats = jnp.concatenate([own_side[HALF:], other_side[HALF:]], 1)
        put(slots * width, across(feats, slots).astype(jnp.bfloat16))


def work_kernel(plan, refs):
    rows = plan.rows
    copies, small = [], []
    if plan.picks:
        adjacency, features, cols, match_one, match_two = [refs[at] for at in plan.sources]
        cols_here, one_rows, two_rows, sems = [refs[at] for at in plan.scratch]
        one_table, two_table = [refs[at] for at in plan.tables]
        width = adjacency.shape[-1]
        small = [start(cols, cols_here, sems.at[2])]
        if plan.first:
            small += [
                start(match_one, one_table, sems.at[0]),
                start(match_two, two_table, sems.at[1]),
            ]
        sides = []
        for i, (pick, (mains, main_at, side, side_at)) in enumerate(zip(plan.picks, plan.targets)):
            tile = tile_at(*pick)
            lanes = pl.ds(pl.multiple_of(tile * width, width), width)
            sides.append(refs[side].at[pl.ds(side_at, HALF)])
            for at, (first, end) in enumerate(pieces_of(rows // width, len(mains))):
                size = (end - first) * width
                copies.append(
                    start(
                        adjacency.at[tile, pl.ds(first * width, size)],
                        refs[mains[at]].at[pl.ds(main_at, size)],
                        sems.at[plan.sems[i] + at],
                    )
                )
            copies.append(
                start(
                    features.at[:, lanes],
                    refs[side].at[pl.ds(side_at + HALF, features.shape[0])],
                    sems.at[plan.sems[i] + len(mains)],
                )
            )
    for i, (own, other) in enumerate(plan.merges):
        tiles = [
            [
                None if main is None else refs[main].at[pl.ds(at, (end - first) * plan.width)]
                for main, (first, end) in zip(mains, pieces_of(rows // plan.width, len(mains)))
            ]
            for mains, at, _, _ in (own, other)
        ]
        ends = [refs[side][at : at + plan.depth - rows, :] for _, _, side, at in (own, other)]

        def wanted(row, base=i * plan.sum_depth):
            return plan.place(base + row) is not None

        def put(row, value, base=i * plan.sum_depth):
            out, at = plan.place(base + row)
            refs[out][pl.ds(at, value.shape[0]), :] = value

        merge_tile(rows // plan.width, plan.width, *tiles, *ends, wanted, put)
    for copy in small:
        copy.wait()
    for i, pick in enumerate(plan.picks):
        compose_maps(
            pick, plan.span, plan.count, cols_here, one_table, two_table, one_rows, two_rows,
            sides[i],
        )
    for copy in copies:
        copy.wait()


class Plan:
    def place(self, row):
        for out, segments in self.outs:
            at = 0
            for first, size in segments:
                if first <= row < first + size:
                    return out, at + row - first
                at += size
        return None


class Work:
    def __init__(self, features, adjacency, cols, match_one, match_two, span):
        self.sources = [in_hbm(x) for x in (adjacency, features, cols, match_one, match_two)]
        self.tables = []
        self.span = span
        self.own, self.other = {}, {}

    def run(self, merges=(), keys=(), leaving=(), apart=(), joint=False, after=(), sums=None):
        adjacency, features, cols, match_one, match_two = self.sources
        rows, width = adjacency.shape[1:]
        plan = Plan()
        plan.rows, plan.depth = rows, rows + HALF + features.shape[0]
        plan.width, plan.sum_depth = width, rows + features.shape[0]
        plan.span, plan.count = self.span, cols.shape[1]
        plan.picks = [(*key, True) for key in leaving] + [(*key, False) for key in keys]
        ins, specs, shapes, scratch = [], [], [], []

        def take(value, spec):
            for place, known in enumerate(ins):
                if known is value:
                    return place
            ins.append(value)
            specs.append(spec)
            return len(ins) - 1

        plan.sources = [take(value, HBM) for value in self.sources] if plan.picks else []
        plan.first = not self.tables
        plan.tables = [take(value, VMEM) for value in self.tables] if plan.picks else []
        if sums is None:
            sums = [[(0, len(merges) * plan.sum_depth)]] if merges else []
        plan.outs = [(None, segments) for segments in sums]

        def needed(i, mains, at):
            first, end = pieces_of(rows // width, len(mains))[at]
            base = i * plan.sum_depth
            return any(plan.place(base + slot * width) for slot in range(first, end))

        plan.merges = [
            [
                (
                    [
                        take(main, VMEM) if needed(i, mains, piece) else None
                        for piece, main in enumerate(mains)
                    ],
                    at,
                    take(side, VMEM),
                    side_at,
                )
                for mains, at, side, side_at in (self.own[key], self.other[key])
            ]
            for i, key in enumerate(merges)
        ]
        for value in after:
            take(value, ANY)

        def give(depth):
            shapes.append(pltpu.VMEM((depth, width), adjacency.dtype))
            return len(ins) + len(shapes) - 1

        plan.outs = [(give(sum(size for _, size in segments)), segments) for segments in sums]
        extra = plan.depth - rows
        if apart:
            ends = len(leaving) * extra
            side = None if joint else give(ends)
            plan.targets = []
            for i, parts in enumerate(apart):
                heights = [(end - first) * width for first, end in pieces_of(rows // width, parts)]
                if i == 0:
                    behind = heights[0] if joint else 0
                    heights[0] += ends if joint else 0
                mains = [give(height) for height in heights]
                side = mains[0] if side is None else side
                plan.targets.append((mains, 0, side, behind + i * extra))
        else:
            mains = [give(plan.depth) for _ in leaving]
            plan.targets = [([main], 0, main, rows) for main in mains]
        if keys:
            pack = give(len(keys) * plan.depth)
            plan.targets += [
                ([pack], i * plan.depth, pack, i * plan.depth + rows) for i in range(len(keys))
            ]
        if plan.first:
            for table in (match_one, match_two):
                plan.tables.append(len(ins) + len(shapes))
                shapes.append(pltpu.VMEM(table.shape, table.dtype))
        plan.sems, total = [], 3
        for mains, _, _, _ in plan.targets:
            plan.sems.append(total)
            total += len(mains) + 1
        if plan.picks:
            scratch = [
                pltpu.SMEM(cols.shape, jnp.int32),
                pltpu.VMEM((HALF, width), jnp.int32),
                pltpu.VMEM((HALF, width), jnp.int32),
                pltpu.SemaphoreType.DMA((total,)),
            ]
        plan.scratch = [len(ins) + len(shapes) + i for i in range(len(scratch))]
        outs = pl.pallas_call(
            lambda *refs: work_kernel(plan, refs),
            out_shape=shapes,
            in_specs=specs,
            out_specs=[VMEM] * len(shapes),
            scratch_shapes=scratch,
            compiler_params=pltpu.CompilerParams(vmem_limit_bytes=LIMIT),
            cost_estimate=LIGHT,
            name="work",
        )(*ins)
        made = {len(ins) + i: value for i, value in enumerate(outs)}
        if plan.first:
            self.tables = [in_vmem(made[at]) for at in plan.tables]
        crossed = {}
        for pick, (mains, main_at, side, side_at) in zip(plan.picks, plan.targets):
            where = self.other if pick[2] else self.own
            for place in (*mains, side):
                if place not in crossed:
                    value = swapped(made[place], "sub") if pick[2] else made[place]
                    crossed[place] = in_vmem(value)
            where[pick[:2]] = ([crossed[main] for main in mains], main_at, crossed[side], side_at)
        return list(outs[: len(sums)] if merges else outs)


def add_kernel(parts, depth, rows, *refs):
    tiles_out, feats_out, total, sems = refs[-4:]
    kept = refs[len(parts)]
    width = kept.shape[-1]
    copies = []
    begin = 0
    listed = []
    for segments, arrived in zip(parts, refs):
        top = begin
        for first, size in segments:
            listed.append((arrived, top, first, size, begin))
            begin += size
    for arrived, top, first, size, begin in listed:
        for tile in range(first // depth, -(-(first + size) // depth)):
            for low, high in ((0, rows), (rows, depth)):
                low, high = max(first, tile * depth + low), min(first + size, tile * depth + high)
                if low >= high:
                    continue
                at = begin + low - first
                value = kept[low:high].astype(jnp.float32)
                value += arrived[at - top : at - top + high - low].astype(jnp.float32)
                total[at : at + high - low] = value.astype(jnp.bfloat16)
                if high - tile * depth > rows:
                    target = feats_out.at[:, pl.ds(tile * width, width)]
                else:
                    target = tiles_out.at[tile, pl.ds(low - tile * depth, high - low)]
                source = total.at[pl.ds(at, high - low)]
                copies.append(start(source, target, sems.at[len(copies)]))
    for copy in copies:
        copy.wait()


def added(parts, depth, rows, arrived, kept, before):
    size, width = sum(part.shape[0] for part in arrived), kept.shape[1]
    quarter = kept.shape[0] // depth
    shapes = (
        jax.ShapeDtypeStruct((quarter, rows, width), jnp.bfloat16),
        jax.ShapeDtypeStruct((depth - rows, quarter * width), jnp.bfloat16),
    )
    return pl.pallas_call(
        functools.partial(add_kernel, parts, depth, rows),
        out_shape=shapes,
        in_specs=[VMEM] * (len(arrived) + 1) + [HBM] * len(before),
        out_specs=(HBM, HBM),
        scratch_shapes=[
            pltpu.VMEM((size, width), jnp.bfloat16),
            pltpu.SemaphoreType.DMA((2 * quarter + sum(map(len, parts)),)),
        ],
        input_output_aliases={len(arrived) + at: at - 1 for at in (1, 2)} if before else {},
        compiler_params=pltpu.CompilerParams(vmem_limit_bytes=LIMIT),
        cost_estimate=LIGHT,
        name="add",
    )(*map(in_vmem, arrived), in_vmem(kept), *before)


def per_device(features, adjacency, col_tiles, match_one, match_two):
    count, slots, width = adjacency.shape[:3]
    feat_count = features.shape[0]
    quarter = count // 4
    span = lax.axis_size("sub") * count
    blocks = adjacency.reshape(count, slots * width, width)
    work = Work(features, blocks, col_tiles.T, match_one, match_two, span)

    send = [(0, piece) for piece in range(quarter)]
    keep = [(1, piece) for piece in range(quarter)]
    rows = slots * width
    depth = rows + feat_count
    half = slots // 2 * width
    first = work.run(leaving=send[:2])
    work.run(keys=send[:2], after=first[:1])
    cut = 3 * depth + 5 * slots // 8 * width
    parts = [
        [(0, half), (rows, feat_count)],
        [(half, rows - half), (depth, depth)],
        [(2 * depth, cut - 2 * depth)],
        [(cut, quarter * depth - cut)],
    ]
    arrived = []

    def merge(keys, which, after):
        base = keys[0][1] * depth
        sums = [[(first - base, size) for first, size in parts[at]] for at in which]
        parcels = work.run(merges=keys, sums=sums, after=after)
        arrived.extend(crossed_over(parcel) for parcel in parcels)
        return parcels

    parcels = merge(send[:1], [0], [])
    parcels = merge(send[:2], [1], parcels)
    work.run(
        keys=send[2:], leaving=send[2:], apart=[1] * (quarter - 2), joint=True,
        after=parcels + arrived[:1],
    )
    parcels = merge(send[2:], [2, 3], [])
    last = work.run(
        keys=keep, leaving=keep, apart=[1] * quarter, joint=True, after=parcels[:1] + arrived[1:2]
    )
    kept = work.run(merges=keep, after=last[:1])[0]
    out = []
    for low, high in ((0, 2), (2, 3), (3, 4)):
        out = added(parts[low:high], depth, rows, arrived[low:high], kept, out)
    return out[0].reshape(quarter, slots, width, width), out[1]


def solution(mesh):
    placed = (
        P(None, ("blk", "sub")),
        P(("blk", "sub"), None, None, None),
        P(("blk", "sub"), None),
        P(),
        P(),
    )
    return jax.shard_map(
        per_device,
        mesh=mesh,
        in_specs=placed,
        out_specs=(P(("blk", "sub"), None, None, None), P(None, ("blk", "sub"))),
        check_vma=False,
    )
```
